32 devices in a mesh: row: 4 (over y, x), col: 8 (over z, core).
Axes of the slice: x: 2, y: 2, z: 4, core: 2. Of those that a mesh axis runs over, the one named last changes fastest.
Arguments:
- bin_features: bfloat16 [1024, 512], P('row'), may hold values from -6 to 6
- w_left: bfloat16 [512, 32], replicated, may hold values from -0.25 to 0.25
- w_right: bfloat16 [512, 32], replicated, may hold values from -0.25 to 0.25
- depth_kernel: float32 [9, 32], replicated, may hold values from -2 to 2
- w_point: bfloat16 [32, 32], replicated, may hold values from -1 to 1
- w_head: bfloat16 [32, 24], replicated, may hold values from -1 to 1
- cotangent: bfloat16 [24, 1024, 1024], P(None, 'row', 'col'), may hold values from -6 to 6
Outputs:
- grad_features: bfloat16 [1024, 512], P('row')
- grad_w_left: float32 [512, 32], replicated
- grad_w_right: float32 [512, 32], replicated
- grad_kernel: float32 [9, 32], replicated
- grad_point: float32 [32, 32], replicated
- grad_head: float32 [32, 24], replicated
The draws below stay inside these ranges and needn't reach their ends.
All inputs are finite; a program needn't handle non-finite values.
Results may differ from the reference program's by a relative error of at most 0.019.
Values may be sent and summed in bfloat16 or wider, within the bound.
A program may use at most 64 MiB of HBM per device.

```python
import math
import jax
import jax.numpy as jnp
from jax import lax

D = 512
CH = 32
HEADS = 24
DILATION_STEP = 4
NB = 1024


def level_of(rng, dims, cuts, least, top_value):
    def one(dim, shards_of):
        heights = jax.random.uniform(jax.random.fold_in(jax.random.fold_in(rng, 6), dim), (shards_of,), jnp.float32, least / len(cuts), top_value / len(cuts))
        return jnp.repeat(jnp.exp(heights), dims[dim] // shards_of).reshape((-1,) + (1,) * (len(dims) - dim - 1))

    gain = one(*cuts[0])
    for cut in cuts[1:]:
        gain = gain * one(*cut)
    return gain


def centred(rng, shape, spread, limit, split=(), held_as=jnp.bfloat16):
    loudness = level_of(rng, shape, split, -0.22, 0.18) if split else 1.0
    result = jax.random.normal(rng, shape, jnp.float32) * spread * loudness
    return jnp.minimum(jnp.maximum(result, -limit), limit).astype(held_as)


def setup_inputs(seed: int = 0) -> dict:
    arg_keys = jax.random.split(jax.random.key(seed), 8)
    return {
        "bin_features": centred(arg_keys[0], (NB, D), 1.0, 6.0, ((0, 4),)),
        "w_left": centred(arg_keys[1], (D, CH), D ** -0.5, 0.25),
        "w_right": centred(arg_keys[2], (D, CH), D ** -0.5, 0.25),
        "depth_kernel": centred(arg_keys[3], (9, CH), 9 ** -0.5, 2.0, (), jnp.float32),
        "w_point": centred(arg_keys[4], (CH, CH), CH ** -0.5, 1.0),
        "w_head": centred(arg_keys[5], (CH, HEADS), CH ** -0.5, 1.0),
        "cotangent": centred(arg_keys[6], (HEADS, NB, NB), 1.0, 6.0, ((1, 4), (2, 8))),
    }


def silu_slope(values):
    logistic = jax.nn.sigmoid(values)
    return logistic * (1.0 + values * (1.0 - logistic))

def rounded(values):
    return lax.optimization_barrier(values.astype(jnp.bfloat16)).astype(jnp.float32)

def reference(bin_features, w_left, w_right, depth_kernel, w_point, w_head, cotangent):
    contact_map_bins = bin_features.shape[0]
    chans = w_left.shape[1]
    head_count = w_head.shape[1]
    grad_scale = 1.0 / math.sqrt(contact_map_bins)
    left_proj = jnp.dot(bin_features, w_left, preferred_element_type=jnp.float32).astype(jnp.bfloat16)
    right_projection = jnp.dot(bin_features, w_right, preferred_element_type=jnp.float32).astype(jnp.bfloat16)
    rows_per_block = math.gcd(contact_map_bins, 128)
    block_count = contact_map_bins // rows_per_block
    border_margin = 2 * DILATION_STEP
    extended_rows = rows_per_block + 2 * DILATION_STEP
    left_pad = jnp.pad(left_proj.astype(jnp.float32), ((border_margin, border_margin), (0, 0))).T
    right_padding = jnp.pad(right_projection.astype(jnp.float32), ((DILATION_STEP, DILATION_STEP), (0, 0))).T
    row_place = jnp.arange(contact_map_bins + 2 * border_margin) - border_margin
    row_valid = jnp.where((row_place >= 0) & (row_place < contact_map_bins), 1.0, 0.0).astype(jnp.float32)
    column_position = jnp.arange(contact_map_bins + 2 * DILATION_STEP) - DILATION_STEP
    col_valid = jnp.where((column_position >= 0) & (column_position < contact_map_bins), 1.0, 0.0).astype(jnp.float32)
    head_padding = jnp.pad(cotangent, ((0, 0), (DILATION_STEP, DILATION_STEP), (0, 0)))
    kernel_taps = depth_kernel.astype(jnp.float32)
    point_weight = w_point.astype(jnp.float32)
    head_weight = w_head.astype(jnp.float32)

    def one_block(totals, row_start):
        kern_acc, pointwise_running_sum, head_running_sum, right_acc = totals
        row_slab = lax.dynamic_slice_in_dim(left_pad, row_start, rows_per_block + 2 * border_margin, 1)
        slab_valid = lax.dynamic_slice_in_dim(row_valid, row_start, rows_per_block + 2 * border_margin, 0)
        extended_pair = rounded((row_slab[:, :, None] + right_padding[:, None, :]) * (slab_valid[:, None] * col_valid[None, :])[None])
        convolved_map = jnp.zeros((chans, extended_rows, contact_map_bins), jnp.float32)
        for kernel_tap_row in range(3):
            for kernel_tap_column in range(3):
                convolved_map = convolved_map + kernel_taps[3 * kernel_tap_row + kernel_tap_column][:, None, None] * extended_pair[:, DILATION_STEP * kernel_tap_row:DILATION_STEP * kernel_tap_row + extended_rows, DILATION_STEP * kernel_tap_column:DILATION_STEP * kernel_tap_column + contact_map_bins]
        hidden_state = rounded(jax.nn.silu(convolved_map))
        mixed_out = jnp.einsum('co,cij->oij', point_weight, hidden_state)
        centre_offset = extended_pair[:, DILATION_STEP:DILATION_STEP + extended_rows, DILATION_STEP:DILATION_STEP + contact_map_bins]
        trunk_matrix = rounded(centre_offset + mixed_out)
        head_weight_block = lax.dynamic_slice_in_dim(head_padding, row_start, extended_rows, 1).astype(jnp.float32)
        trunk_gradient = rounded(grad_scale * jnp.einsum('ch,hij->cij', head_weight, head_weight_block))
        grad_hidden = jnp.einsum('co,oij->cij', point_weight, trunk_gradient)
        convolved_gradient = rounded(grad_hidden * silu_slope(convolved_map))
        padded_convolved_gradient = jnp.pad(convolved_gradient, ((0, 0), (0, 0), (DILATION_STEP, DILATION_STEP)))
        inner_convolved = convolved_gradient[:, DILATION_STEP:DILATION_STEP + rows_per_block]
        backward_pass = jnp.zeros((chans, rows_per_block, contact_map_bins), jnp.float32)
        kern_terms = []
        for kernel_tap_row in range(3):
            for kernel_tap_column in range(3):
                backward_pass = backward_pass + kernel_taps[3 * kernel_tap_row + kernel_tap_column][:, None, None] * padded_convolved_gradient[:, DILATION_STEP * (2 - kernel_tap_row):DILATION_STEP * (2 - kernel_tap_row) + rows_per_block, DILATION_STEP * (2 - kernel_tap_column):DILATION_STEP * (2 - kernel_tap_column) + contact_map_bins]
                shifted_window = extended_pair[:, DILATION_STEP + DILATION_STEP * kernel_tap_row:DILATION_STEP + DILATION_STEP * kernel_tap_row + rows_per_block, DILATION_STEP * kernel_tap_column:DILATION_STEP * kernel_tap_column + contact_map_bins]
                kern_terms.append(lax.optimization_barrier(jnp.sum(inner_convolved * shifted_window, axis=(1, 2))))
        pair_gradient = trunk_gradient[:, DILATION_STEP:DILATION_STEP + rows_per_block] + backward_pass
        left_out = lax.optimization_barrier(jnp.sum(pair_gradient, axis=2)).T
        right_acc = right_acc + lax.optimization_barrier(jnp.sum(pair_gradient, axis=1))
        pointwise_running_sum = pointwise_running_sum + jnp.einsum('fsk,gsk->fg', hidden_state[:, DILATION_STEP:DILATION_STEP + rows_per_block], trunk_gradient[:, DILATION_STEP:DILATION_STEP + rows_per_block])
        head_running_sum = head_running_sum + jnp.einsum('ydq,gdq->yg', trunk_matrix[:, DILATION_STEP:DILATION_STEP + rows_per_block], head_weight_block[:, DILATION_STEP:DILATION_STEP + rows_per_block])
        kern_acc = kern_acc + jnp.stack(kern_terms)
        return ((kern_acc, pointwise_running_sum, head_running_sum, right_acc), left_out)
    starts = (jnp.arange(block_count) * rows_per_block).astype(jnp.int32)
    initial = (jnp.zeros((9, chans), jnp.float32), jnp.zeros((chans, chans), jnp.float32), jnp.zeros((chans, head_count), jnp.float32), jnp.zeros((chans, contact_map_bins), jnp.float32))
    totals, left_blocks = lax.scan(one_block, initial, starts)
    kern_acc, pointwise_running_sum, head_running_sum, right_acc = totals
    grad_left = left_blocks.reshape(contact_map_bins, chans).astype(jnp.bfloat16)
    grad_right = right_acc.T.astype(jnp.bfloat16)
    grad_features = (jnp.dot(grad_left, w_left.T, preferred_element_type=jnp.float32) + jnp.dot(grad_right, w_right.T, preferred_element_type=jnp.float32)).astype(jnp.bfloat16)
    grad_w_left = grad_scale * jnp.dot(bin_features.T, grad_left, preferred_element_type=jnp.float32)
    grad_w_right = grad_scale * jnp.dot(bin_features.T, grad_right, preferred_element_type=jnp.float32)
    return (grad_features, grad_w_left, grad_w_right, grad_scale * kern_acc, grad_scale * pointwise_running_sum, grad_scale * head_running_sum)
```

```python
import functools
import math

import jax
import jax.numpy as jnp
from jax import lax
from jax.experimental import pallas as pl
from jax.experimental.pallas import tpu as pltpu
from jax.sharding import PartitionSpec as P

STEP = 4
BF = jnp.bfloat16
F32 = jnp.float32
HI = lax.Precision.HIGHEST
GR = 16


def iota(shape, dim):
    return lax.broadcasted_iota(jnp.int32, shape, dim)


def split(x):
    hi = x.astype(BF)
    return hi, (x - hi.astype(F32)).astype(BF)


def dotf(a, b, contract=((1,), (0,)), precision=None):
    return lax.dot_general(a, b, (contract, ((), ())), precision=precision, preferred_element_type=F32)


def tile_kernel(scale, lext, rext, dk, wp, wh, cot, plx, prx, small,
                qs, ns, k2, cm, es, ecol, ecx, rs, cs, gcs, hid, xs, zl, zr):
    ch, heads = wh.shape
    tr, tc = cot.shape[1:]
    groups = tr // GR
    cg, hg = ch * GR, heads * GR
    row, col = lax.axis_index("row"), lax.axis_index("col")
    row_first, row_last = row == 0, row == lax.axis_size("row") - 1
    col_first, col_last = col == 0, col == lax.axis_size("col") - 1
    taps = [[dk[3 * a + b : 3 * a + b + 1, :] for b in range(3)] for a in range(3)]

    def edge(first, last, pos, length):
        return ((pos < STEP) & first) | ((pos >= length - STEP) & last)

    l_sh = [lext[8 + STEP * (a - 1) : 8 + STEP * (a - 1) + tr, :] for a in range(3)]
    r_sh = [rext[8 + STEP * (b - 1) : 8 + STEP * (b - 1) + tc, :] for b in range(3)]
    a1 = sum(l_sh[a] * (taps[a][0] + taps[a][1] + taps[a][2]) for a in range(3))
    da0 = sum(l_sh[a] * taps[a][0] for a in range(3))
    da2 = sum(l_sh[a] * taps[a][2] for a in range(3))
    da = -jnp.where(col_first, da0, jnp.where(col_last, da2, jnp.zeros_like(da2)))
    b1 = sum(r_sh[b] * (taps[0][b] + taps[1][b] + taps[2][b]) for b in range(3))
    db0 = sum(r_sh[b] * taps[0][b] for b in range(3))
    db2 = sum(r_sh[b] * taps[2][b] for b in range(3))
    db = -jnp.where(row_first, db0, jnp.where(row_last, db2, jnp.zeros_like(db2)))
    rind = jnp.where(edge(row_first, row_last, iota((tr, 2 * ch), 0), tr), 1.0, 0.0).astype(BF)
    qs[...] = jnp.concatenate(
        [*split(0.5 * a1), *split(0.5 * da), jnp.ones((tr, 2 * ch), BF), rind], axis=1)
    b_parts = [p.astype(F32) for p in (*split(0.5 * b1), *split(0.5 * db))]
    ns[4 * ch :, :] = jnp.concatenate(b_parts, axis=1).T.astype(BF)
    ns[: 2 * ch, :] = jnp.ones((2 * ch, tc), BF)
    ns[2 * ch : 4 * ch, :] = jnp.where(
        edge(col_first, col_last, iota((2 * ch, tc), 1), tc), 1.0, 0.0).astype(BF)
    cm[...] = jnp.where(iota((cg, 8 * ch), 0) // GR == iota((cg, 8 * ch), 1) % ch, 1.0, 0.0).astype(BF)

    w2 = (0.5 * scale * dotf(wp[...], wh[...])).astype(BF)
    e_r = jnp.where(iota((cg, ch), 0) // GR == iota((cg, ch), 1), 1.0, 0.0).astype(BF)
    e_c = jnp.where(iota((heads, hg), 1) // GR == iota((heads, hg), 0), 1.0, 0.0).astype(BF)
    w2r = dotf(e_r, w2).astype(BF)
    same = iota((cg, hg), 0) % GR == iota((cg, hg), 1) % GR
    k2[...] = jnp.where(same, dotf(w2r, e_c), 0.0).astype(BF)

    jj, part = iota((tc, 4 * ch), 0), iota((tc, 4 * ch), 1) // ch
    drop = ((part == 0) & (jj < STEP) & col_first) | ((part == 2) & (jj >= tc - STEP) & col_last)
    es[0] = jnp.where(drop | (part == 3), 0.0, 1.0).astype(BF)
    es[1] = jnp.where(part == 3, 1.0, 0.0).astype(BF)
    pr, ci = iota((4 * ch, cg), 0), iota((4 * ch, cg), 1)
    mine = (pr % ch == ci // GR) & (pr // ch < 3)
    top = (pr // ch == 0) & (ci % GR < STEP) & row_first
    low = (pr // ch == 2) & (ci % GR >= GR - STEP) & row_last
    ecol[0] = jnp.where(mine & ~top, 1.0, 0.0).astype(BF)
    ecol[1] = jnp.where(mine, 1.0, 0.0).astype(BF)
    ecol[2] = jnp.where(mine & ~low, 1.0, 0.0).astype(BF)
    ecx[...] = jnp.where(
        iota((4 * ch, hg), 0) == 3 * ch + iota((4 * ch, hg), 1) // GR, 1.0, 0.0).astype(BF)
    cs[...] = jnp.zeros_like(cs)

    chunk = 128
    lane_c = iota((1, 1, 4 * ch), 2) % ch

    def group(g, carry):
        start = pl.multiple_of(g * GR, GR)
        lanes = pl.ds(pl.multiple_of(g * tc, 128), tc)
        x = cot[:, pl.ds(start, GR), :].reshape(hg, tc)
        xs[:, lanes] = x
        q = qs[pl.ds(start, GR), :]
        total = jnp.zeros((GR, 4 * ch), F32)
        for k in range(cg // chunk):
            rows = slice(k * chunk, (k + 1) * chunk)
            n = chunk // GR
            m = (cm[rows, :].reshape(n, GR, 8 * ch) * q[None]).reshape(chunk, 8 * ch)
            u = dotf(m, ns[...])
            gh = dotf(k2[rows, :], x)
            t = jnp.tanh(u)
            p = 1.0 + t
            h = u * p
            gc = (gh * (p + h - h * t)).astype(BF)
            hid[rows, lanes] = h.astype(BF)
            gcs[rows, :] = gc
            y = dotf(gc, es[0]).reshape(n, GR, 4 * ch)
            pick = iota((n, 1, 4 * ch), 0) + k * n == lane_c
            total = total + jnp.sum(jnp.where(pick, y, 0.0), axis=0)
        y = dotf(x, es[1]).reshape(heads, GR, 4 * ch)
        total = total + jnp.sum(jnp.where(iota((heads, 1, 4 * ch), 0) == lane_c, y, 0.0), axis=0)
        rs[pl.ds(start, GR), :] = total
        kind = jnp.where(g == 0, 0, jnp.where(g == groups - 1, 2, 1))
        cs[...] += dotf(ecol[kind], gcs[...]) + dotf(ecx[...], x)
        return carry

    lax.fori_loop(0, groups, group, 0)

    prod = dotf(hid[...], xs[...], ((1,), (1,)))
    prod = jnp.sum(jnp.where(same, prod, 0.0).reshape(ch, GR, hg), axis=1)
    e_h = jnp.where(iota((hg, ch), 0) // GR == iota((hg, ch), 1), 1.0, 0.0)
    hc = dotf(prod, e_h, precision=HI)
    cst = cs[...].T
    rsv = rs[...]
    pc = dotf(l_sh[1], rsv[:, 3 * ch :], ((0,), (0,)), HI) + dotf(r_sh[1], cst[:, 3 * ch :], ((0,), (0,)), HI)
    small[:ch, :] = jnp.concatenate([hc, pc, jnp.zeros((ch, 2 * ch), F32)], axis=1)
    rows_out = []
    zero_l, zero_r = jnp.zeros((tr, ch), F32), jnp.zeros((tc, ch), F32)
    for a in range(3):
        rows_out.append(jnp.sum(jnp.concatenate([l_sh[a]] * 3 + [zero_l], axis=1) * rsv, axis=0, keepdims=True))
    for b in range(3):
        rows_out.append(jnp.sum(jnp.concatenate([r_sh[b]] * 3 + [zero_r], axis=1) * cst, axis=0, keepdims=True))
    small[ch:, :] = jnp.concatenate(rows_out + [jnp.zeros((2, 4 * ch), F32)], axis=0)

    eye = iota((ch, ch), 0) == iota((ch, ch), 1)
    whs = scale * dotf(jnp.where(iota((ch, heads), 0) == iota((ch, heads), 1), 1.0, 0.0).astype(BF), wh[...], ((1,), (1,)))
    zc = jnp.zeros((ch, ch), F32)

    def spread(tap):
        blocks = [[jnp.where(eye, tap(n, m), 0.0) for m in range(3)] + [zc] for n in range(3)]
        blocks.append([zc, zc, zc, whs])
        return jnp.concatenate([jnp.concatenate(b, axis=1) for b in blocks], axis=0)

    for sums, z, out, length, weights in (
        (rsv, zl, plx, tr, spread(lambda b, a: taps[a][b])),
        (cst, zr, prx, tc, spread(lambda a, b: taps[a][b])),
    ):
        z[:16, :] = jnp.zeros((16, 4 * ch), F32)
        z[16 + length :, :] = jnp.zeros((16, 4 * ch), F32)
        z[16 : 16 + length, :] = dotf(sums, weights, precision=HI)
        ext = z[8 : 24 + length, 3 * ch :]
        for n in range(3):
            ext = ext + z[12 - STEP * n : 28 - STEP * n + length, n * ch : (n + 1) * ch]
        out[...] = ext


def tile(scale, lext, rext, dk, wp, wh, cot):
    ch, heads = wh.shape
    tr, tc = cot.shape[1:]
    cg, hg, groups = ch * GR, heads * GR, tr // GR
    vm = pl.BlockSpec(memory_space=pltpu.VMEM)
    return pl.pallas_call(
        functools.partial(tile_kernel, scale),
        out_shape=(
            jax.ShapeDtypeStruct((tr + 16, ch), F32),
            jax.ShapeDtypeStruct((tc + 16, ch), F32),
            jax.ShapeDtypeStruct((ch + 8, 4 * ch), F32),
        ),
        in_specs=[vm] * 6,
        out_specs=(vm,) * 3,
        scratch_shapes=[
            pltpu.VMEM((tr, 8 * ch), BF),
            pltpu.VMEM((8 * ch, tc), BF),
            pltpu.VMEM((cg, hg), BF),
            pltpu.VMEM((cg, 8 * ch), BF),
            pltpu.VMEM((2, tc, 4 * ch), BF),
            pltpu.VMEM((3, 4 * ch, cg), BF),
            pltpu.VMEM((4 * ch, hg), BF),
            pltpu.VMEM((tr, 4 * ch), F32),
            pltpu.VMEM((4 * ch, tc), F32),
            pltpu.VMEM((cg, tc), BF),
            pltpu.VMEM((cg, groups * tc), BF),
            pltpu.VMEM((hg, groups * tc), BF),
            pltpu.VMEM((tr + 32, 4 * ch), F32),
            pltpu.VMEM((tc + 32, 4 * ch), F32),
        ],
        compiler_params=pltpu.CompilerParams(vmem_limit_bytes=48 * 1024 * 1024),
    )(lext, rext, dk, wp, wh, cot)


def body(bin_features, w_left, w_right, depth_kernel, w_point, w_head, cotangent):
    ch, heads = w_head.shape
    tr, tc = cotangent.shape[1:]
    nb = tr * lax.axis_size("row")
    scale = 1.0 / math.sqrt(nb)
    row, col = lax.axis_index("row"), lax.axis_index("col")
    feats = lax.all_gather(bin_features, "row", axis=0, tiled=True)
    both = dotf(feats, jnp.concatenate([w_left, w_right], axis=1)).astype(BF).astype(F32)
    both = jnp.pad(both, ((8, 8), (0, 0)))
    lext = lax.dynamic_slice(both, (row * tr, 0), (tr + 16, ch))
    rext = lax.dynamic_slice(both, (col * tc, ch), (tc + 16, ch))
    plx, prx, small = tile(scale, lext, rext, depth_kernel, w_point, w_head, cotangent)
    full_l = lax.dynamic_update_slice(jnp.zeros((nb + 16, ch), F32), plx, (row * tr, 0))
    full_r = lax.dynamic_update_slice(jnp.zeros((nb + 16, ch), F32), prx, (col * tc, 0))
    full = jnp.concatenate([full_l, full_r], axis=1)
    full, small = lax.psum((full, small), ("row", "col"))
    grads = full[8 : 8 + nb].astype(BF)
    grad_features = dotf(
        lax.dynamic_slice(grads, (row * tr, 0), (tr, 2 * ch)),
        jnp.concatenate([w_left, w_right], axis=1), ((1,), (1,))).astype(BF)
    gw = scale * dotf(feats, grads, ((0,), (0,)))
    hc, pc = small[:ch, :heads], small[:ch, ch : ch + heads]
    gk = small[ch : ch + 3, : 3 * ch].reshape(3, 3, ch) + small[ch + 3 : ch + 6, : 3 * ch].reshape(3, 3, ch).transpose(1, 0, 2)
    grad_point = scale * scale * dotf(hc, w_head.astype(F32), ((1,), (1,)), HI)
    grad_head = scale * (pc + dotf(w_point.astype(F32), hc, ((0,), (0,)), HI))
    return grad_features, gw[:, :ch], gw[:, ch:], scale * gk.reshape(9, ch), grad_point, grad_head


def solution(mesh):
    return jax.shard_map(
        body,
        mesh=mesh,
        in_specs=(P("row", None), P(), P(), P(), P(), P(), P(None, "row", "col")),
        out_specs=(P("row", None), P(), P(), P(), P(), P()),
        check_vma=False,
    )
```

```python
import functools
import math

import jax
import jax.numpy as jnp
from jax import lax
from jax.experimental import pallas as pl
from jax.experimental.pallas import tpu as pltpu
from jax.sharding import PartitionSpec as P

STEP = 4
BF = jnp.bfloat16
F32 = jnp.float32
HI = lax.Precision.HIGHEST
GR = 16


def iota(shape, dim):
    return lax.broadcasted_iota(jnp.int32, shape, dim)


def split(x):
    hi = x.astype(BF)
    return hi, (x - hi.astype(F32)).astype(BF)


def dotf(a, b, contract=((1,), (0,)), precision=None):
    return lax.dot_general(a, b, (contract, ((), ())), precision=precision, preferred_element_type=F32)


MESH = pl.DeviceIdType.MESH


def pack(x):
    n = x.shape[0] // 4
    return jnp.concatenate([x[k * n : (k + 1) * n] for k in range(4)], axis=1)


def unpack(x):
    n = x.shape[1] // 4
    return jnp.concatenate([x[:, k * n : (k + 1) * n] for k in range(4)], axis=0)


def tile_kernel(scale, feats, wl, wr, dk, wp, wh, cot, gf_out, gwl_out, gwr_out, gk_out, gp_out, gh_out,
                lext, rext, plx, prx, small, qs, ns, k2, cm, es, ecol, ecx, rs, cs, gcs, hid, xs, zl, zr,
                proj, lbuf, rbuf, colsend, colrecv, rowsend, rowrecv, halosend, halorecv,
                agsend, agrecv, spsend, sprecv, sfin, gwsend, gwrecv, window,
                rseg_send, rseg_recv, lseg_send, lseg_recv, c1s, c1r, r1s, r1r, h1s, h1r,
                c2s, c2r, r2s, r2r, c3s, c3r, r3s, r3r, local_sem):
    ch, heads = wh.shape
    tr, tc = cot.shape[1:]
    groups = tr // GR
    cg, hg = ch * GR, heads * GR
    row, col = lax.axis_index("row"), lax.axis_index("col")
    row_first, row_last = row == 0, row == lax.axis_size("row") - 1
    col_first, col_last = col == 0, col == lax.axis_size("col") - 1
    taps = [[dk[3 * a + b : 3 * a + b + 1, :] for b in range(3)] for a in range(3)]

    def edge(first, last, pos, length):
        return ((pos < STEP) & first) | ((pos >= length - STEP) & last)

    n_row, n_col = lax.axis_size("row"), lax.axis_size("col")
    nb = tr * n_row
    row_mates = [lax.rem(row + k, n_row) for k in range(1, n_row)]
    col_mates = [lax.rem(col + k, n_col) for k in range(1, n_col)]

    lbuf[...] = jnp.zeros_like(lbuf)
    halorecv[...] = jnp.zeros_like(halorecv)
    for first, count in ((0, 16), (16 + tc, 16)):
        rbuf[first : first + count, :] = jnp.zeros((count, 4 * ch), BF)
    barrier = pltpu.get_barrier_semaphore()
    for m in row_mates:
        pl.semaphore_signal(barrier, inc=1, device_id=(m, col), device_id_type=MESH)
    for m in col_mates:
        pl.semaphore_signal(barrier, inc=1, device_id=(row, m), device_id_type=MESH)

    weights = jnp.concatenate([wl[...], wr[...], jnp.zeros((wl.shape[0], 2 * ch), BF)], axis=1)
    proj[...] = dotf(feats[...], weights).astype(BF)
    pl.semaphore_wait(barrier, n_row + n_col - 2)

    def remote(src, dst, send, recv, device):
        return pltpu.make_async_remote_copy(
            src_ref=src, dst_ref=dst, send_sem=send, recv_sem=recv, device_id=device, device_id_type=MESH)

    up = remote(proj.at[pl.ds(0, 16)], lbuf.at[1], lseg_send.at[0], lseg_recv.at[1], (row - 1, col))
    down = remote(proj.at[pl.ds(tr - 16, 16)], lbuf.at[0], lseg_send.at[1], lseg_recv.at[0], (row + 1, col))
    pl.when(row > 0)(up.start)
    pl.when(row < n_row - 1)(down.start)
    segments = []
    for k, (offset, first, count) in enumerate(((-16, 0, 16), (0, 16, tc), (tc, 16 + tc, 16))):
        bin0 = col * tc + offset
        inside = (bin0 >= 0) & (bin0 < nb)
        owner = lax.div(bin0 + nb, tr) - n_row
        local = pl.multiple_of(lax.rem(bin0 + nb, tr), 16)
        src = proj.at[pl.ds(local, count)]
        dst = rbuf.at[pl.ds(first, count)]
        own = inside & (owner == row)
        copies = [remote(src, dst, rseg_send.at[k, i], rseg_recv.at[k], (m, col)) for i, m in enumerate(row_mates)]
        keep = pltpu.make_async_copy(src, dst, local_sem.at[k])
        segments.append((inside, own, copies, keep))

        @pl.when(own)
        def _(copies=copies, keep=keep):
            for c in copies:
                c.start()
            keep.start()

    cm[...] = jnp.where(iota((cg, 8 * ch), 0) // GR == iota((cg, 8 * ch), 1) % ch, 1.0, 0.0).astype(BF)

    w2 = (0.5 * scale * dotf(wp[...], wh[...])).astype(BF)
    e_r = jnp.where(iota((cg, ch), 0) // GR == iota((cg, ch), 1), 1.0, 0.0).astype(BF)
    e_c = jnp.where(iota((heads, hg), 1) // GR == iota((heads, hg), 0), 1.0, 0.0).astype(BF)
    w2r = dotf(e_r, w2).astype(BF)
    same = iota((cg, hg), 0) % GR == iota((cg, hg), 1) % GR
    k2[...] = jnp.where(same, dotf(w2r, e_c), 0.0).astype(BF)

    jj, part = iota((tc, 4 * ch), 0), iota((tc, 4 * ch), 1) // ch
    drop = ((part == 0) & (jj < STEP) & col_first) | ((part == 2) & (jj >= tc - STEP) & col_last)
    es[0] = jnp.where(drop | (part == 3), 0.0, 1.0).astype(BF)
    es[1] = jnp.where(part == 3, 1.0, 0.0).astype(BF)
    pr, ci = iota((4 * ch, cg), 0), iota((4 * ch, cg), 1)
    mine = (pr % ch == ci // GR) & (pr // ch < 3)
    top = (pr // ch == 0) & (ci % GR < STEP) & row_first
    low = (pr // ch == 2) & (ci % GR >= GR - STEP) & row_last
    ecol[0] = jnp.where(mine & ~top, 1.0, 0.0).astype(BF)
    ecol[1] = jnp.where(mine, 1.0, 0.0).astype(BF)
    ecol[2] = jnp.where(mine & ~low, 1.0, 0.0).astype(BF)
    ecx[...] = jnp.where(
        iota((4 * ch, hg), 0) == 3 * ch + iota((4 * ch, hg), 1) // GR, 1.0, 0.0).astype(BF)
    for inside, own, copies, keep in segments:

        @pl.when(own)
        def _(copies=copies, keep=keep):
            keep.wait()
            for c in copies:
                c.wait_send()

        @pl.when(inside & jnp.logical_not(own))
        def _(copies=copies):
            copies[0].wait_recv()

    @pl.when(row > 0)
    def _():
        up.wait_send()
        down.wait_recv()

    @pl.when(row < n_row - 1)
    def _():
        down.wait_send()
        up.wait_recv()

    lext[0:16, :] = lbuf[0, :, :ch].astype(F32)
    lext[16 : 16 + tr, :] = proj[:, :ch].astype(F32)
    lext[16 + tr :, :] = lbuf[1, :, :ch].astype(F32)
    rext[...] = rbuf[:, ch : 2 * ch].astype(F32)

    l_sh = [lext[16 + STEP * (a - 1) : 16 + STEP * (a - 1) + tr, :] for a in range(3)]
    r_sh = [rext[16 + STEP * (b - 1) : 16 + STEP * (b - 1) + tc, :] for b in range(3)]
    a1 = sum(l_sh[a] * (taps[a][0] + taps[a][1] + taps[a][2]) for a in range(3))
    da0 = sum(l_sh[a] * taps[a][0] for a in range(3))
    da2 = sum(l_sh[a] * taps[a][2] for a in range(3))
    da = -jnp.where(col_first, da0, jnp.where(col_last, da2, jnp.zeros_like(da2)))
    b1 = sum(r_sh[b] * (taps[0][b] + taps[1][b] + taps[2][b]) for b in range(3))
    db0 = sum(r_sh[b] * taps[0][b] for b in range(3))
    db2 = sum(r_sh[b] * taps[2][b] for b in range(3))
    db = -jnp.where(row_first, db0, jnp.where(row_last, db2, jnp.zeros_like(db2)))
    rind = jnp.where(edge(row_first, row_last, iota((tr, 2 * ch), 0), tr), 1.0, 0.0).astype(BF)
    qs[...] = jnp.concatenate(
        [*split(0.5 * a1), *split(0.5 * da), jnp.ones((tr, 2 * ch), BF), rind], axis=1)
    b_parts = [p.astype(F32) for p in (*split(0.5 * b1), *split(0.5 * db))]
    ns[4 * ch :, :] = jnp.concatenate(b_parts, axis=1).T.astype(BF)
    ns[: 2 * ch, :] = jnp.ones((2 * ch, tc), BF)
    ns[2 * ch : 4 * ch, :] = jnp.where(
        edge(col_first, col_last, iota((2 * ch, tc), 1), tc), 1.0, 0.0).astype(BF)
    cs[...] = jnp.zeros_like(cs)

    chunk = 128
    lane_c = iota((1, 1, 4 * ch), 2) % ch

    def group(g, carry):
        start = pl.multiple_of(g * GR, GR)
        lanes = pl.ds(pl.multiple_of(g * tc, 128), tc)
        x = cot[:, pl.ds(start, GR), :].reshape(hg, tc)
        xs[:, lanes] = x
        q = qs[pl.ds(start, GR), :]
        total = jnp.zeros((GR, 4 * ch), F32)
        for k in range(cg // chunk):
            rows = slice(k * chunk, (k + 1) * chunk)
            n = chunk // GR
            m = (cm[rows, :].reshape(n, GR, 8 * ch) * q[None]).reshape(chunk, 8 * ch)
            u = dotf(m, ns[...])
            gh = dotf(k2[rows, :], x)
            t = jnp.tanh(u)
            p = 1.0 + t
            h = u * p
            gc = (gh * (p + h - h * t)).astype(BF)
            hid[rows, lanes] = h.astype(BF)
            gcs[rows, :] = gc
            y = dotf(gc, es[0]).reshape(n, GR, 4 * ch)
            pick = iota((n, 1, 4 * ch), 0) + k * n == lane_c
            total = total + jnp.sum(jnp.where(pick, y, 0.0), axis=0)
        y = dotf(x, es[1]).reshape(heads, GR, 4 * ch)
        total = total + jnp.sum(jnp.where(iota((heads, 1, 4 * ch), 0) == lane_c, y, 0.0), axis=0)
        rs[pl.ds(start, GR), :] = total
        kind = (g + groups - 1) // groups + g // (groups - 1)
        cs[...] += dotf(ecol[kind], gcs[...]) + dotf(ecx[...], x)
        return carry

    lax.fori_loop(0, groups, group, 0)

    prod = dotf(hid[...], xs[...], ((1,), (1,)))
    prod = jnp.sum(jnp.where(same, prod, 0.0).reshape(ch, GR, hg), axis=1)
    e_h = jnp.where(iota((hg, ch), 0) // GR == iota((hg, ch), 1), 1.0, 0.0)
    hc = dotf(prod, e_h, precision=HI)
    cst = cs[...].T
    rsv = rs[...]
    pc = dotf(l_sh[1], rsv[:, 3 * ch :], ((0,), (0,)), HI) + dotf(r_sh[1], cst[:, 3 * ch :], ((0,), (0,)), HI)
    small[:ch, :] = jnp.concatenate([hc, pc, jnp.zeros((ch, 2 * ch), F32)], axis=1)
    rows_out = []
    zero_l, zero_r = jnp.zeros((tr, ch), F32), jnp.zeros((tc, ch), F32)
    for a in range(3):
        rows_out.append(jnp.sum(jnp.concatenate([l_sh[a]] * 3 + [zero_l], axis=1) * rsv, axis=0, keepdims=True))
    for b in range(3):
        rows_out.append(jnp.sum(jnp.concatenate([r_sh[b]] * 3 + [zero_r], axis=1) * cst, axis=0, keepdims=True))
    small[ch : ch + 8, :] = jnp.concatenate(rows_out + [jnp.zeros((2, 4 * ch), F32)], axis=0)
    small[ch + 8 :, :] = jnp.zeros((ch - 8, 4 * ch), F32)

    eye = iota((ch, ch), 0) == iota((ch, ch), 1)
    whs = scale * dotf(jnp.where(iota((ch, heads), 0) == iota((ch, heads), 1), 1.0, 0.0).astype(BF), wh[...], ((1,), (1,)))
    zc = jnp.zeros((ch, ch), F32)

    def spread(tap):
        blocks = [[jnp.where(eye, tap(n, m), 0.0) for m in range(3)] + [zc] for n in range(3)]
        blocks.append([zc, zc, zc, whs])
        return jnp.concatenate([jnp.concatenate(b, axis=1) for b in blocks], axis=0)

    for sums, z, out, length, weights in (
        (rsv, zl, plx, tr, spread(lambda b, a: taps[a][b])),
        (cst, zr, prx, tc, spread(lambda a, b: taps[a][b])),
    ):
        z[:16, :] = jnp.zeros((16, 4 * ch), F32)
        z[16 + length :, :] = jnp.zeros((16, 4 * ch), F32)
        z[16 : 16 + length, :] = dotf(sums, weights, precision=HI)
        ext = z[8 : 24 + length, 3 * ch :]
        for n in range(3):
            ext = ext + z[12 - STEP * n : 28 - STEP * n + length, n * ch : (n + 1) * ch]
        out[...] = ext

    lanes = 4 * ch
    pp, sp = tr // 4 // n_col, 2 * ch // n_col
    colsend[:, :pp, :] = pack(plx[8 : 8 + tr, :]).reshape(n_col, pp, lanes)
    colsend[:, pp:, :] = small[...].reshape(n_col, sp, lanes)
    pad = jnp.zeros((8, 3 * ch), F32)
    halosend[0] = jnp.concatenate([plx[:8, :], pad], axis=1)
    halosend[1] = jnp.concatenate([plx[8 + tr :, :], pad], axis=1)
    pr = (tc + 16) // 4
    rowsend[...] = pack(prx[...])

    def to_col(src, dst, send, recv):
        return [remote(src(m), dst.at[col], send.at[m], recv.at[col], (row, m)) for m in col_mates]

    def to_row(src, dst, send, recv):
        return [remote(src, dst.at[row], send.at[m], recv.at[row], (m, col)) for m in row_mates]

    def from_col(src, dst, send, recv):
        return [remote(src(m), dst.at[m], send.at[m], recv.at[m], (row, m)) for m in col_mates]

    def from_row(src, dst, send, recv):
        return [remote(src, dst.at[m], send.at[m], recv.at[m], (m, col)) for m in row_mates]

    def start(copies):
        for c in copies:
            c.start()

    def arrived(copies):
        for c in copies:
            c.wait_recv()

    def sent(copies):
        for c in copies:
            c.wait_send()

    hup = remote(halosend.at[0], halorecv.at[1], h1s.at[0], h1r.at[1], (row - 1, col))
    hdown = remote(halosend.at[1], halorecv.at[0], h1s.at[1], h1r.at[0], (row + 1, col))
    p1c = (lambda m: colsend.at[m], colrecv, c1s, c1r)
    p1r = (rowsend, rowrecv, r1s, r1r)
    s1c, s1r = to_col(*p1c), to_row(*p1r)
    start(s1c)
    start(s1r)
    pl.when(row > 0)(hup.start)
    pl.when(row < n_row - 1)(hdown.start)
    arrived(from_col(*p1c))
    piece = colsend[col]
    for m in col_mates:
        piece = piece + colrecv[m]
    spsend[...] = piece[pp:]
    p2r = (spsend, sprecv, r2s, r2r)
    s2r = to_row(*p2r)
    start(s2r)
    arrived(from_row(*p1r))
    right = rowsend[...]
    for m in row_mates:
        right = right + rowrecv[m]

    @pl.when(row > 0)
    def _():
        hup.wait_send()
        hdown.wait_recv()

    @pl.when(row < n_row - 1)
    def _():
        hdown.wait_send()
        hup.wait_recv()

    fill = [jnp.zeros((agsend.shape[0] - pp - 4 - pr, lanes), F32)] if agsend.shape[0] > pp + 4 + pr else []
    agsend[...] = jnp.concatenate(
        [right, pack(halorecv[0, :, :ch]), pack(halorecv[1, :, :ch]), piece[:pp]] + fill, axis=0).astype(BF)
    p2c = (lambda m: agsend, agrecv, c2s, c2r)
    s2c = to_col(*p2c)
    start(s2c)
    sent(s1c)
    sent(s1r)
    arrived(from_row(*p2r))
    total = spsend[...]
    for m in row_mates:
        total = total + sprecv[m]
    sfin[col] = total
    p3c = (lambda m: sfin.at[col], sfin, c3s, c3r)
    s3c = to_col(*p3c)
    start(s3c)
    arrived(from_col(*p2c))
    sent(s2c)
    agrecv[col] = agsend[...]
    gl = unpack(jnp.concatenate([agrecv[m, pr + 4 : pr + 4 + pp, :].astype(F32) for m in range(n_col)], axis=0))
    halo = sum(agrecv[m, pr : pr + 4, :].astype(F32) for m in range(n_col))
    gl = jnp.concatenate([gl[:8] + unpack(halo[:2]), gl[8:-8], gl[-8:] + unpack(halo[2:])], axis=0)
    window[...] = jnp.zeros_like(window)
    for k in range(tr // tc + 2):
        m = lax.div(row * tr, tc) - 1 + k

        @pl.when((m >= 0) & (m < n_col))
        def _(m=m, k=k):
            window[k * tc : k * tc + tc + 16, :] += unpack(agrecv[m, :pr, :].astype(F32))

    gr = window[tc + 8 : tc + 8 + tr, :]
    glb, grb = gl.astype(BF), gr.astype(BF)
    both = jnp.concatenate([gl, gr, jnp.zeros((tr, 2 * ch), F32)], axis=1).T[: 2 * ch].astype(BF)
    part = scale * dotf(both, feats[...])

    gwsend[...] = part.astype(BF)
    p3r = (gwsend, gwrecv, r3s, r3r)
    s3r = to_row(*p3r)
    start(s3r)
    gf_out[...] = (dotf(glb, wl[...], ((1,), (1,))) + dotf(grb, wr[...], ((1,), (1,)))).astype(BF)
    arrived(from_col(*p3c))
    sent(s3c)
    sent(s2r)
    full = jnp.concatenate([sfin[m] for m in range(n_col)], axis=0)
    hc, pc = full[:ch, :heads], full[:ch, ch : ch + heads]
    for a in range(3):
        for b in range(3):
            gk_out[3 * a + b : 3 * a + b + 1, :] = scale * (
                full[ch + a : ch + a + 1, b * ch : (b + 1) * ch]
                + full[ch + 3 + b : ch + 4 + b, a * ch : (a + 1) * ch])
    gp_out[...] = scale * scale * dotf(hc, wh[...].astype(F32), ((1,), (1,)), HI)
    gh_out[...] = scale * (pc + dotf(wp[...].astype(F32), hc, ((0,), (0,)), HI))
    arrived(from_row(*p3r))
    for m in row_mates:
        part = part + gwrecv[m].astype(F32)
    part = part.T
    gwl_out[...] = part[:, :ch]
    gwr_out[...] = part[:, ch:]
    sent(s3r)


def body(bin_features, w_left, w_right, depth_kernel, w_point, w_head, cotangent):
    ch, heads = w_head.shape
    tr, tc = cotangent.shape[1:]
    n_row, n_col = lax.axis_size("row"), lax.axis_size("col")
    scale = 1.0 / math.sqrt(tr * n_row)
    cg, hg, groups = ch * GR, heads * GR, tr // GR
    d, lanes = w_left.shape[0], 4 * ch
    pp, sp, pr = tr // 4 // n_col, 2 * ch // n_col, (tc + 16) // 4
    ag = -(-(pp + 4 + pr) // 16) * 16
    vm = pl.BlockSpec(memory_space=pltpu.VMEM)
    dma = pltpu.SemaphoreType.DMA
    return pl.pallas_call(
        functools.partial(tile_kernel, scale),
        out_shape=(
            jax.ShapeDtypeStruct((tr, d), BF),
            jax.ShapeDtypeStruct((d, ch), F32),
            jax.ShapeDtypeStruct((d, ch), F32),
            jax.ShapeDtypeStruct((9, ch), F32),
            jax.ShapeDtypeStruct((ch, ch), F32),
            jax.ShapeDtypeStruct((ch, heads), F32),
        ),
        in_specs=[vm] * 7,
        out_specs=(vm,) * 6,
        scratch_shapes=[
            pltpu.VMEM((tr + 32, ch), F32),
            pltpu.VMEM((tc + 32, ch), F32),
            pltpu.VMEM((tr + 16, ch), F32),
            pltpu.VMEM((tc + 16, ch), F32),
            pltpu.VMEM((2 * ch, lanes), F32),
            pltpu.VMEM((tr, 8 * ch), BF),
            pltpu.VMEM((8 * ch, tc), BF),
            pltpu.VMEM((cg, hg), BF),
            pltpu.VMEM((cg, 8 * ch), BF),
            pltpu.VMEM((2, tc, 4 * ch), BF),
            pltpu.VMEM((3, 4 * ch, cg), BF),
            pltpu.VMEM((4 * ch, hg), BF),
            pltpu.VMEM((tr, 4 * ch), F32),
            pltpu.VMEM((4 * ch, tc), F32),
            pltpu.VMEM((cg, tc), BF),
            pltpu.VMEM((cg, groups * tc), BF),
            pltpu.VMEM((hg, groups * tc), BF),
            pltpu.VMEM((tr + 32, 4 * ch), F32),
            pltpu.VMEM((tc + 32, 4 * ch), F32),
            pltpu.VMEM((tr, lanes), BF),
            pltpu.VMEM((2, 16, lanes), BF),
            pltpu.VMEM((tc + 32, lanes), BF),
            pltpu.VMEM((n_col, pp + sp, lanes), F32),
            pltpu.VMEM((n_col, pp + sp, lanes), F32),
            pltpu.VMEM((pr, lanes), F32),
            pltpu.VMEM((n_row, pr, lanes), F32),
            pltpu.VMEM((2, 8, lanes), F32),
            pltpu.VMEM((2, 8, lanes), F32),
            pltpu.VMEM((ag, lanes), BF),
            pltpu.VMEM((n_col, ag, lanes), BF),
            pltpu.VMEM((sp, lanes), F32),
            pltpu.VMEM((n_row, sp, lanes), F32),
            pltpu.VMEM((n_col, sp, lanes), F32),
            pltpu.VMEM((2 * ch, d), BF),
            pltpu.VMEM((n_row, 2 * ch, d), BF),
            pltpu.VMEM((tr + 2 * tc + 16, ch), F32),
            dma((3, n_row)), dma((3,)), dma((2,)), dma((2,)),
            dma((n_col,)), dma((n_col,)), dma((n_row,)), dma((n_row,)), dma((2,)), dma((2,)),
            dma((n_col,)), dma((n_col,)), dma((n_row,)), dma((n_row,)),
            dma((n_col,)), dma((n_col,)), dma((n_row,)), dma((n_row,)),
            dma((3,)),
        ],
        compiler_params=pltpu.CompilerParams(
            vmem_limit_bytes=48 * 1024 * 1024, collective_id=0, has_side_effects=True),
    )(bin_features, w_left, w_right, depth_kernel, w_point, w_head, cotangent)


def solution(mesh):
    return jax.shard_map(
        body,
        mesh=mesh,
        in_specs=(P("row", None), P(), P(), P(), P(), P(), P(None, "row", "col")),
        out_specs=(P("row", None), P(), P(), P(), P(), P()),
        check_vma=False,
    )
```

```python
import functools
import math

import jax
import jax.numpy as jnp
from jax import lax
from jax.experimental import pallas as pl
from jax.experimental.pallas import tpu as pltpu
from jax.sharding import PartitionSpec as P

STEP = 4
BF = jnp.bfloat16
F32 = jnp.float32
HI = lax.Precision.HIGHEST
GR = 16


def iota(shape, dim):
    return lax.broadcasted_iota(jnp.int32, shape, dim)


def split(x):
    hi = x.astype(BF)
    return hi, (x - hi.astype(F32)).astype(BF)


def dotf(a, b, contract=((1,), (0,)), precision=None):
    return lax.dot_general(a, b, (contract, ((), ())), precision=precision, preferred_element_type=F32)


MESH = pl.DeviceIdType.MESH


def pack(x):
    n = x.shape[0] // 4
    return jnp.concatenate([x[k * n : (k + 1) * n] for k in range(4)], axis=1)


def unpack(x):
    n = x.shape[1] // 4
    return jnp.concatenate([x[:, k * n : (k + 1) * n] for k in range(4)], axis=0)


def tile_kernel(scale, feats_hbm, wl_hbm, wr_hbm, dk_hbm, wp_hbm, wh_hbm, cot_hbm,
                gf_out, gwl_out, gwr_out, gk_out, gp_out, gh_out,
                feats, wl, wr, dk, wp, wh, cot, load_sem, ghs,
                lext, rext, plx, prx, small, qs, ns, k2, cm, es, ecol, ecx, rs, cs, gcs, hid, xs, zl, zr,
                proj, lbuf, rbuf, colsend, colrecv, rowsend, rowrecv, halosend, halorecv,
                agsend, agrecv, spsend, sprecv, sfin, gwsend, gwrecv, window,
                rseg_send, rseg_recv, lseg_send, lseg_recv, c1s, c1r, r1s, r1r, h1s, h1r,
                c2s, c2r, r2s, r2r, c3s, c3r, r3s, r3r, local_sem):
    loads = [pltpu.make_async_copy(src, dst, load_sem.at[k]) for k, (src, dst) in enumerate((
        (feats_hbm, feats), (wl_hbm, wl), (wr_hbm, wr), (dk_hbm, dk), (wp_hbm, wp), (wh_hbm, wh), (cot_hbm, cot)))]
    for copy in loads:
        copy.start()
    heads, ch = wh.shape
    tr, tc = cot.shape[1:]
    groups = tr // GR
    cg, hg = ch * GR, heads * GR
    row, col = lax.axis_index("row"), lax.axis_index("col")
    row_first, row_last = row == 0, row == lax.axis_size("row") - 1
    col_first, col_last = col == 0, col == lax.axis_size("col") - 1
    def edge(first, last, pos, length):
        return ((pos < STEP) & first) | ((pos >= length - STEP) & last)

    n_row, n_col = lax.axis_size("row"), lax.axis_size("col")
    nb = tr * n_row
    row_mates = [lax.rem(row + k, n_row) for k in range(1, n_row)]
    col_mates = [lax.rem(col + k, n_col) for k in range(1, n_col)]

    lbuf[...] = jnp.zeros_like(lbuf)
    halorecv[...] = jnp.zeros_like(halorecv)
    for first, count in ((0, 16), (16 + tc, 16)):
        rbuf[first : first + count, :] = jnp.zeros((count, 4 * ch), BF)
    barrier = pltpu.get_barrier_semaphore()
    for m in row_mates:
        pl.semaphore_signal(barrier, inc=1, device_id=(m, col), device_id_type=MESH)
    for m in col_mates:
        pl.semaphore_signal(barrier, inc=1, device_id=(row, m), device_id_type=MESH)

    for copy in loads[:6]:
        copy.wait()
    taps = [[dk[3 * a + b : 3 * a + b + 1, :] for b in range(3)] for a in range(3)]

    weights = jnp.concatenate([wl[...], wr[...], jnp.zeros((2 * ch, wl.shape[1]), BF)], axis=0)
    proj[...] = dotf(feats[...], weights, ((1,), (1,))).astype(BF)
    pl.semaphore_wait(barrier, n_row + n_col - 2)

    def remote(src, dst, send, recv, device):
        return pltpu.make_async_remote_copy(
            src_ref=src, dst_ref=dst, send_sem=send, recv_sem=recv, device_id=device, device_id_type=MESH)

    up = remote(proj.at[pl.ds(0, 16)], lbuf.at[1], lseg_send.at[0], lseg_recv.at[1], (row - 1, col))
    down = remote(proj.at[pl.ds(tr - 16, 16)], lbuf.at[0], lseg_send.at[1], lseg_recv.at[0], (row + 1, col))
    pl.when(row > 0)(up.start)
    pl.when(row < n_row - 1)(down.start)
    segments = []
    for k, (offset, first, count) in enumerate(((-16, 0, 16), (0, 16, tc), (tc, 16 + tc, 16))):
        bin0 = col * tc + offset
        inside = (bin0 >= 0) & (bin0 < nb)
        owner = lax.div(bin0 + nb, tr) - n_row
        local = pl.multiple_of(lax.rem(bin0 + nb, tr), 16)
        src = proj.at[pl.ds(local, count)]
        dst = rbuf.at[pl.ds(first, count)]
        own = inside & (owner == row)
        copies = [remote(src, dst, rseg_send.at[k, i], rseg_recv.at[k], (m, col)) for i, m in enumerate(row_mates)]
        keep = pltpu.make_async_copy(src, dst, local_sem.at[k])
        segments.append((inside, own, copies, keep))

        @pl.when(own)
        def _(copies=copies, keep=keep):
            for c in copies:
                c.start()
            keep.start()

    cm[...] = jnp.where(iota((cg, 8 * ch), 0) // GR == iota((cg, 8 * ch), 1) % ch, 1.0, 0.0).astype(BF)

    w2 = (0.5 * scale * dotf(wp[...], wh[...], ((1,), (1,)))).astype(BF)
    e_r = jnp.where(iota((cg, ch), 0) // GR == iota((cg, ch), 1), 1.0, 0.0).astype(BF)
    e_c = jnp.where(iota((heads, hg), 1) // GR == iota((heads, hg), 0), 1.0, 0.0).astype(BF)
    w2r = dotf(e_r, w2).astype(BF)
    same = iota((cg, hg), 0) % GR == iota((cg, hg), 1) % GR
    k2[...] = jnp.where(same, dotf(w2r, e_c), 0.0).astype(BF)

    jj, part = iota((2 * tc, 8 * ch), 0), iota((2 * tc, 8 * ch), 1)
    paired = jj // tc == part // (4 * ch)
    jj, part = jj % tc, part % (4 * ch) // ch
    drop = ((part == 0) & (jj < STEP) & col_first) | ((part == 2) & (jj >= tc - STEP) & col_last)
    es[0] = jnp.where(paired & ~drop & (part != 3), 1.0, 0.0).astype(BF)
    es[1] = jnp.where(paired & (part == 3), 1.0, 0.0).astype(BF)
    pr, ci = iota((4 * ch, cg), 0), iota((4 * ch, cg), 1)
    mine = (pr % ch == ci // GR) & (pr // ch < 3)
    top = (pr // ch == 0) & (ci % GR < STEP) & row_first
    low = (pr // ch == 2) & (ci % GR >= GR - STEP) & row_last
    ecol[0] = jnp.where(mine & ~top, 1.0, 0.0).astype(BF)
    ecol[1] = jnp.where(mine, 1.0, 0.0).astype(BF)
    ecol[2] = jnp.where(mine & ~low, 1.0, 0.0).astype(BF)
    ecx[...] = jnp.where(
        iota((4 * ch, hg), 0) == 3 * ch + iota((4 * ch, hg), 1) // GR, 1.0, 0.0).astype(BF)
    cs[...] = jnp.zeros_like(cs)
    lane_c = iota((1, 1, 8 * ch), 2) % ch
    loads[6].wait()

    def ahead(g, carry):
        start = pl.multiple_of(g * 2 * GR, 2 * GR)
        lanes = pl.ds(pl.multiple_of(g * 2 * tc, 256), 2 * tc)
        x = jnp.concatenate(
            [cot[:, pl.ds(start + k * GR, GR), :].reshape(hg, tc) for k in range(2)], axis=1)
        xs[:, lanes] = x
        ghs[:, lanes] = dotf(k2[...], x)
        y = dotf(x, es[1]).reshape(heads, GR, 8 * ch)
        y = jnp.sum(jnp.where(iota((heads, 1, 8 * ch), 0) == lane_c, y, 0.0), axis=0)
        rs[pl.ds(start, GR), :] = y[:, : 4 * ch]
        rs[pl.ds(start + GR, GR), :] = y[:, 4 * ch :]
        y = dotf(ecx[...], x)
        cs[...] += y[:, :tc] + y[:, tc:]
        return carry

    lax.fori_loop(0, groups // 2, ahead, 0)

    for inside, own, copies, keep in segments:

        @pl.when(own)
        def _(copies=copies, keep=keep):
            keep.wait()
            for c in copies:
                c.wait_send()

        @pl.when(inside & jnp.logical_not(own))
        def _(copies=copies):
            copies[0].wait_recv()

    @pl.when(row > 0)
    def _():
        up.wait_send()
        down.wait_recv()

    @pl.when(row < n_row - 1)
    def _():
        down.wait_send()
        up.wait_recv()

    lext[0:16, :] = lbuf[0, :, :ch].astype(F32)
    lext[16 : 16 + tr, :] = proj[:, :ch].astype(F32)
    lext[16 + tr :, :] = lbuf[1, :, :ch].astype(F32)
    rext[...] = rbuf[:, ch : 2 * ch].astype(F32)

    l_sh = [lext[16 + STEP * (a - 1) : 16 + STEP * (a - 1) + tr, :] for a in range(3)]
    r_sh = [rext[16 + STEP * (b - 1) : 16 + STEP * (b - 1) + tc, :] for b in range(3)]
    a1 = sum(l_sh[a] * (taps[a][0] + taps[a][1] + taps[a][2]) for a in range(3))
    da0 = sum(l_sh[a] * taps[a][0] for a in range(3))
    da2 = sum(l_sh[a] * taps[a][2] for a in range(3))
    da = -jnp.where(col_first, da0, jnp.where(col_last, da2, jnp.zeros_like(da2)))
    b1 = sum(r_sh[b] * (taps[0][b] + taps[1][b] + taps[2][b]) for b in range(3))
    db0 = sum(r_sh[b] * taps[0][b] for b in range(3))
    db2 = sum(r_sh[b] * taps[2][b] for b in range(3))
    db = -jnp.where(row_first, db0, jnp.where(row_last, db2, jnp.zeros_like(db2)))
    rind = jnp.where(edge(row_first, row_last, iota((tr, 2 * ch), 0), tr), 1.0, 0.0).astype(BF)
    qs[...] = jnp.concatenate(
        [*split(0.5 * a1), *split(0.5 * da), jnp.ones((tr, 2 * ch), BF), rind], axis=1)
    b_parts = [p.astype(F32) for p in (*split(0.5 * b1), *split(0.5 * db))]
    ns[4 * ch :, :] = jnp.concatenate(b_parts, axis=1).T.astype(BF)
    ns[: 2 * ch, :] = jnp.ones((2 * ch, tc), BF)
    ns[2 * ch : 4 * ch, :] = jnp.where(
        edge(col_first, col_last, iota((2 * ch, tc), 1), tc), 1.0, 0.0).astype(BF)

    chunk = 128
    n = chunk // GR

    def group(g, carry):
        start = pl.multiple_of(g * 2 * GR, 2 * GR)
        q = [qs[pl.ds(start + j * GR, GR), :] for j in range(2)]
        total = jnp.zeros((GR, 8 * ch), F32)
        for k in range(cg // chunk):
            rows = slice(k * chunk, (k + 1) * chunk)
            mask = cm[rows, :].reshape(n, GR, 8 * ch)
            for j in range(2):
                lanes = pl.ds(pl.multiple_of(g * 2 * tc + j * tc, 128), tc)
                u = dotf((mask * q[j][None]).reshape(chunk, 8 * ch), ns[...])
                t = jnp.tanh(u)
                p = 1.0 + t
                h = u * p
                hid[rows, lanes] = h.astype(BF)
                gcs[rows, j * tc : (j + 1) * tc] = (ghs[rows, lanes] * (p + h - h * t)).astype(BF)
            y = dotf(gcs[rows, :], es[0]).reshape(n, GR, 8 * ch)
            total = total + jnp.sum(jnp.where(iota((n, 1, 8 * ch), 0) + k * n == lane_c, y, 0.0), axis=0)
        rs[pl.ds(start, GR), :] += total[:, : 4 * ch]
        rs[pl.ds(start + GR, GR), :] += total[:, 4 * ch :]
        first = (g + groups - 1) // groups
        last = g // (groups // 2 - 1) + 1
        cs[...] += dotf(ecol[first], gcs[:, :tc]) + dotf(ecol[last], gcs[:, tc:])
        return carry

    lax.fori_loop(0, groups // 2, group, 0)

    prod = dotf(hid[...], xs[...], ((1,), (1,)))
    prod = jnp.sum(jnp.where(same, prod, 0.0).reshape(ch, GR, hg), axis=1)
    e_h = jnp.where(iota((hg, ch), 0) // GR == iota((hg, ch), 1), 1.0, 0.0)
    hc = dotf(prod, e_h, precision=HI)
    cst = cs[...].T
    rsv = rs[...]
    pc = dotf(l_sh[1], rsv[:, 3 * ch :], ((0,), (0,)), HI) + dotf(r_sh[1], cst[:, 3 * ch :], ((0,), (0,)), HI)
    small[:ch, :] = jnp.concatenate([hc, pc, jnp.zeros((ch, 2 * ch), F32)], axis=1)
    rows_out = []
    zero_l, zero_r = jnp.zeros((tr, ch), F32), jnp.zeros((tc, ch), F32)
    for a in range(3):
        rows_out.append(jnp.sum(jnp.concatenate([l_sh[a]] * 3 + [zero_l], axis=1) * rsv, axis=0, keepdims=True))
    for b in range(3):
        rows_out.append(jnp.sum(jnp.concatenate([r_sh[b]] * 3 + [zero_r], axis=1) * cst, axis=0, keepdims=True))
    small[ch : ch + 8, :] = jnp.concatenate(rows_out + [jnp.zeros((2, 4 * ch), F32)], axis=0)
    small[ch + 8 :, :] = jnp.zeros((ch - 8, 4 * ch), F32)

    eye = iota((ch, ch), 0) == iota((ch, ch), 1)
    whs = scale * jnp.concatenate([wh[...].astype(F32), jnp.zeros((ch - heads, ch), F32)], axis=0)
    zc = jnp.zeros((ch, ch), F32)

    def spread(tap):
        blocks = [[jnp.where(eye, tap(n, m), 0.0) for m in range(3)] + [zc] for n in range(3)]
        blocks.append([zc, zc, zc, whs])
        return jnp.concatenate([jnp.concatenate(b, axis=1) for b in blocks], axis=0)

    for sums, z, out, length, weights in (
        (rsv, zl, plx, tr, spread(lambda b, a: taps[a][b])),
        (cst, zr, prx, tc, spread(lambda a, b: taps[a][b])),
    ):
        z[:16, :] = jnp.zeros((16, 4 * ch), F32)
        z[16 + length :, :] = jnp.zeros((16, 4 * ch), F32)
        z[16 : 16 + length, :] = dotf(sums, weights, precision=HI)
        ext = z[8 : 24 + length, 3 * ch :]
        for n in range(3):
            ext = ext + z[12 - STEP * n : 28 - STEP * n + length, n * ch : (n + 1) * ch]
        out[...] = ext

    lanes = 4 * ch
    pp, sp = tr // 4 // n_col, 2 * ch // n_col
    colsend[:, :pp, :] = pack(plx[8 : 8 + tr, :]).reshape(n_col, pp, lanes)
    colsend[:, pp:, :] = small[...].reshape(n_col, sp, lanes)
    pad = jnp.zeros((8, 3 * ch), F32)
    halosend[0] = jnp.concatenate([plx[:8, :], pad], axis=1)
    halosend[1] = jnp.concatenate([plx[8 + tr :, :], pad], axis=1)
    pr = (tc + 16) // 4
    rowsend[...] = pack(prx[...])

    def to_col(src, dst, send, recv):
        return [remote(src(m), dst.at[col], send.at[m], recv.at[col], (row, m)) for m in col_mates]

    def to_row(src, dst, send, recv):
        return [remote(src, dst.at[row], send.at[m], recv.at[row], (m, col)) for m in row_mates]

    def from_col(src, dst, send, recv):
        return [remote(src(m), dst.at[m], send.at[m], recv.at[m], (row, m)) for m in col_mates]

    def from_row(src, dst, send, recv):
        return [remote(src, dst.at[m], send.at[m], recv.at[m], (m, col)) for m in row_mates]

    def start(copies):
        for c in copies:
            c.start()

    def arrived(copies):
        for c in copies:
            c.wait_recv()

    def sent(copies):
        for c in copies:
            c.wait_send()

    hup = remote(halosend.at[0], halorecv.at[1], h1s.at[0], h1r.at[1], (row - 1, col))
    hdown = remote(halosend.at[1], halorecv.at[0], h1s.at[1], h1r.at[0], (row + 1, col))
    p1c = (lambda m: colsend.at[m], colrecv, c1s, c1r)
    p1r = (rowsend, rowrecv, r1s, r1r)
    s1c, s1r = to_col(*p1c), to_row(*p1r)
    start(s1c)
    start(s1r)
    pl.when(row > 0)(hup.start)
    pl.when(row < n_row - 1)(hdown.start)
    arrived(from_col(*p1c))
    piece = colsend[col]
    for m in col_mates:
        piece = piece + colrecv[m]
    spsend[...] = piece[pp:]
    p2r = (spsend, sprecv, r2s, r2r)
    s2r = to_row(*p2r)
    start(s2r)
    arrived(from_row(*p1r))
    right = rowsend[...]
    for m in row_mates:
        right = right + rowrecv[m]

    @pl.when(row > 0)
    def _():
        hup.wait_send()
        hdown.wait_recv()

    @pl.when(row < n_row - 1)
    def _():
        hdown.wait_send()
        hup.wait_recv()

    fill = [jnp.zeros((agsend.shape[0] - pp - 4 - pr, lanes), F32)] if agsend.shape[0] > pp + 4 + pr else []
    agsend[...] = jnp.concatenate(
        [right, pack(halorecv[0, :, :ch]), pack(halorecv[1, :, :ch]), piece[:pp]] + fill, axis=0).astype(BF)
    p2c = (lambda m: agsend, agrecv, c2s, c2r)
    s2c = to_col(*p2c)
    start(s2c)
    sent(s1c)
    sent(s1r)
    arrived(from_row(*p2r))
    total = spsend[...]
    for m in row_mates:
        total = total + sprecv[m]
    sfin[col] = total
    p3c = (lambda m: sfin.at[col], sfin, c3s, c3r)
    s3c = to_col(*p3c)
    start(s3c)
    arrived(from_col(*p2c))
    sent(s2c)
    agrecv[col] = agsend[...]
    gl = unpack(jnp.concatenate([agrecv[m, pr + 4 : pr + 4 + pp, :].astype(F32) for m in range(n_col)], axis=0))
    halo = sum(agrecv[m, pr : pr + 4, :].astype(F32) for m in range(n_col))
    gl = jnp.concatenate([gl[:8] + unpack(halo[:2]), gl[8:-8], gl[-8:] + unpack(halo[2:])], axis=0)
    window[...] = jnp.zeros_like(window)
    for k in range(tr // tc + 2):
        m = lax.div(row * tr, tc) - 1 + k

        @pl.when((m >= 0) & (m < n_col))
        def _(m=m, k=k):
            window[k * tc : k * tc + tc + 16, :] += unpack(agrecv[m, :pr, :].astype(F32))

    gr = window[tc + 8 : tc + 8 + tr, :]
    glb, grb = gl.astype(BF), gr.astype(BF)
    both = jnp.concatenate([gl, gr, jnp.zeros((tr, 2 * ch), F32)], axis=1).T[: 2 * ch].astype(BF)
    part = scale * dotf(both, feats[...])

    gwsend[...] = part.astype(BF)
    p3r = (gwsend, gwrecv, r3s, r3r)
    s3r = to_row(*p3r)
    start(s3r)
    gf_out[...] = (dotf(glb, wl[...]) + dotf(grb, wr[...])).astype(BF)
    arrived(from_col(*p3c))
    sent(s3c)
    sent(s2r)
    full = jnp.concatenate([sfin[m] for m in range(n_col)], axis=0)
    hc, pc = full[:ch, :heads], full[:ch, ch : ch + heads]
    for a in range(3):
        for b in range(3):
            gk_out[3 * a + b : 3 * a + b + 1, :] = scale * (
                full[ch + a : ch + a + 1, b * ch : (b + 1) * ch]
                + full[ch + 3 + b : ch + 4 + b, a * ch : (a + 1) * ch])
    gp_out[...] = scale * scale * dotf(hc, wh[...].astype(F32), precision=HI)
    gh_out[...] = (scale * (pc + dotf(wp[...].astype(F32), hc, ((0,), (0,)), HI))).T
    arrived(from_row(*p3r))
    for m in row_mates:
        part = part + gwrecv[m].astype(F32)
    gwl_out[...] = part[:ch]
    gwr_out[...] = part[ch:]
    sent(s3r)


def body(bin_features, w_left, w_right, depth_kernel, w_point, w_head, cotangent):
    ch, heads = w_head.shape
    tr, tc = cotangent.shape[1:]
    n_row, n_col = lax.axis_size("row"), lax.axis_size("col")
    scale = 1.0 / math.sqrt(tr * n_row)
    cg, hg, groups = ch * GR, heads * GR, tr // GR
    d, lanes = w_left.shape[0], 4 * ch
    pp, sp, pr = tr // 4 // n_col, 2 * ch // n_col, (tc + 16) // 4
    ag = -(-(pp + 4 + pr) // 16) * 16
    vm = pl.BlockSpec(memory_space=pltpu.VMEM)
    dma = pltpu.SemaphoreType.DMA
    operands = (bin_features, w_left.T, w_right.T, depth_kernel, w_point, w_head.T, cotangent)
    gf, gwl, gwr, gk, gp, gh = pl.pallas_call(
        functools.partial(tile_kernel, scale),
        out_shape=(
            jax.ShapeDtypeStruct((tr, d), BF),
            jax.ShapeDtypeStruct((ch, d), F32),
            jax.ShapeDtypeStruct((ch, d), F32),
            jax.ShapeDtypeStruct((9, ch), F32),
            jax.ShapeDtypeStruct((ch, ch), F32),
            jax.ShapeDtypeStruct((heads, ch), F32),
        ),
        in_specs=[pl.BlockSpec(memory_space=pltpu.HBM)] * 7,
        out_specs=(vm,) * 6,
        scratch_shapes=[
            *(pltpu.VMEM(v.shape, v.dtype) for v in operands),
            dma((7,)),
            pltpu.VMEM((cg, groups * tc), F32),
            pltpu.VMEM((tr + 32, ch), F32),
            pltpu.VMEM((tc + 32, ch), F32),
            pltpu.VMEM((tr + 16, ch), F32),
            pltpu.VMEM((tc + 16, ch), F32),
            pltpu.VMEM((2 * ch, lanes), F32),
            pltpu.VMEM((tr, 8 * ch), BF),
            pltpu.VMEM((8 * ch, tc), BF),
            pltpu.VMEM((cg, hg), BF),
            pltpu.VMEM((cg, 8 * ch), BF),
            pltpu.VMEM((2, 2 * tc, 8 * ch), BF),
            pltpu.VMEM((3, 4 * ch, cg), BF),
            pltpu.VMEM((4 * ch, hg), BF),
            pltpu.VMEM((tr, 4 * ch), F32),
            pltpu.VMEM((4 * ch, tc), F32),
            pltpu.VMEM((cg, 2 * tc), BF),
            pltpu.VMEM((cg, groups * tc), BF),
            pltpu.VMEM((hg, groups * tc), BF),
            pltpu.VMEM((tr + 32, 4 * ch), F32),
            pltpu.VMEM((tc + 32, 4 * ch), F32),
            pltpu.VMEM((tr, lanes), BF),
            pltpu.VMEM((2, 16, lanes), BF),
            pltpu.VMEM((tc + 32, lanes), BF),
            pltpu.VMEM((n_col, pp + sp, lanes), F32),
            pltpu.VMEM((n_col, pp + sp, lanes), F32),
            pltpu.VMEM((pr, lanes), F32),
            pltpu.VMEM((n_row, pr, lanes), F32),
            pltpu.VMEM((2, 8, lanes), F32),
            pltpu.VMEM((2, 8, lanes), F32),
            pltpu.VMEM((ag, lanes), BF),
            pltpu.VMEM((n_col, ag, lanes), BF),
            pltpu.VMEM((sp, lanes), F32),
            pltpu.VMEM((n_row, sp, lanes), F32),
            pltpu.VMEM((n_col, sp, lanes), F32),
            pltpu.VMEM((2 * ch, d), BF),
            pltpu.VMEM((n_row, 2 * ch, d), BF),
            pltpu.VMEM((tr + 2 * tc + 16, ch), F32),
            dma((3, n_row)), dma((3,)), dma((2,)), dma((2,)),
            dma((n_col,)), dma((n_col,)), dma((n_row,)), dma((n_row,)), dma((2,)), dma((2,)),
            dma((n_col,)), dma((n_col,)), dma((n_row,)), dma((n_row,)),
            dma((n_col,)), dma((n_col,)), dma((n_row,)), dma((n_row,)),
            dma((3,)),
        ],
        compiler_params=pltpu.CompilerParams(
            vmem_limit_bytes=63 * 1024 * 1024, collective_id=0, has_side_effects=True),
    )(*operands)
    return gf, gwl.T, gwr.T, gk, gp, gh.T


def solution(mesh):
    return jax.shard_map(
        body,
        mesh=mesh,
        in_specs=(P("row", None), P(), P(), P(), P(), P(), P(None, "row", "col")),
        out_specs=(P("row", None), P(), P(), P(), P(), P()),
        check_vma=False,
    )
```

```python
import functools
import math

import jax
import jax.numpy as jnp
from jax import lax
from jax.experimental import pallas as pl
from jax.experimental.pallas import tpu as pltpu
from jax.sharding import PartitionSpec as P

STEP = 4
BF = jnp.bfloat16
F32 = jnp.float32
HI = lax.Precision.HIGHEST
GR = 16


def iota(shape, dim):
    return lax.broadcasted_iota(jnp.int32, shape, dim)


def split(x):
    hi = x.astype(BF)
    return hi, (x - hi.astype(F32)).astype(BF)


def dotf(a, b, contract=((1,), (0,)), precision=None):
    return lax.dot_general(a, b, (contract, ((), ())), precision=precision, preferred_element_type=F32)


MESH = pl.DeviceIdType.MESH


def pack(x):
    n = x.shape[0] // 4
    return jnp.concatenate([x[k * n : (k + 1) * n] for k in range(4)], axis=1)


def unpack(x):
    n = x.shape[1] // 4
    return jnp.concatenate([x[:, k * n : (k + 1) * n] for k in range(4)], axis=0)


def tile_kernel(scale, feats_hbm, wl_hbm, wr_hbm, dk_hbm, wp_hbm, wh_hbm, cot_hbm,
                gf_out, gwl_out, gwr_out, gk_out, gp_out, gh_out,
                feats, wl, wr, dk, wp, wh, cot, load_sem, ghs,
                lext, rext, plx, prx, small, qs, ns, k2, cm, es, ecol, ecx, rs, cs, gcs, hid, xs, zl, zr,
                proj, lbuf, rbuf, colsend, colrecv, rowsend, rowrecv, halosend, halorecv,
                smsend, smrecv, m1s, m1r,
                agsend, agrecv, spsend, sprecv, sfin, gwsend, gwrecv, window,
                rseg_send, rseg_recv, lseg_send, lseg_recv, c1s, c1r, r1s, r1r, h1s, h1r,
                c2s, c2r, r2s, r2r, c3s, c3r, r3s, r3r, local_sem):
    loads = [pltpu.make_async_copy(src, dst, load_sem.at[k]) for k, (src, dst) in enumerate((
        (feats_hbm, feats), (wl_hbm, wl), (wr_hbm, wr), (dk_hbm, dk), (wp_hbm, wp), (wh_hbm, wh), (cot_hbm, cot)))]
    for copy in loads:
        copy.start()
    heads, ch = wh.shape
    tr, tc = cot.shape[1:]
    groups = tr // GR
    cg, hg = ch * GR, heads * GR
    row, col = lax.axis_index("row"), lax.axis_index("col")
    row_first, row_last = row == 0, row == lax.axis_size("row") - 1
    col_first, col_last = col == 0, col == lax.axis_size("col") - 1
    def edge(first, last, pos, length):
        return ((pos < STEP) & first) | ((pos >= length - STEP) & last)

    n_row, n_col = lax.axis_size("row"), lax.axis_size("col")
    nb = tr * n_row
    row_mates = [lax.rem(row + k, n_row) for k in range(1, n_row)]
    col_mates = [lax.rem(col + k, n_col) for k in range(1, n_col)]

    lbuf[...] = jnp.zeros_like(lbuf)
    halorecv[...] = jnp.zeros_like(halorecv)
    for first, count in ((0, 16), (16 + tc, 16)):
        rbuf[first : first + count, :] = jnp.zeros((count, 4 * ch), BF)
    barrier = pltpu.get_barrier_semaphore()
    for m in row_mates:
        pl.semaphore_signal(barrier, inc=1, device_id=(m, col), device_id_type=MESH)
    for m in col_mates:
        pl.semaphore_signal(barrier, inc=1, device_id=(row, m), device_id_type=MESH)

    for copy in loads[:6]:
        copy.wait()
    taps = [[dk[3 * a + b : 3 * a + b + 1, :] for b in range(3)] for a in range(3)]

    weights = jnp.concatenate([wl[...], wr[...], jnp.zeros((2 * ch, wl.shape[1]), BF)], axis=0)
    proj[...] = dotf(feats[...], weights, ((1,), (1,))).astype(BF)
    pl.semaphore_wait(barrier, n_row + n_col - 2)

    def remote(src, dst, send, recv, device):
        return pltpu.make_async_remote_copy(
            src_ref=src, dst_ref=dst, send_sem=send, recv_sem=recv, device_id=device, device_id_type=MESH)

    up = remote(proj.at[pl.ds(0, 16)], lbuf.at[1], lseg_send.at[0], lseg_recv.at[1], (row - 1, col))
    down = remote(proj.at[pl.ds(tr - 16, 16)], lbuf.at[0], lseg_send.at[1], lseg_recv.at[0], (row + 1, col))
    pl.when(row > 0)(up.start)
    pl.when(row < n_row - 1)(down.start)
    segments = []
    for k, (offset, first, count) in enumerate(((-16, 0, 16), (0, 16, tc), (tc, 16 + tc, 16))):
        bin0 = col * tc + offset
        inside = (bin0 >= 0) & (bin0 < nb)
        owner = lax.div(bin0 + nb, tr) - n_row
        local = pl.multiple_of(lax.rem(bin0 + nb, tr), 16)
        src = proj.at[pl.ds(local, count)]
        dst = rbuf.at[pl.ds(first, count)]
        own = inside & (owner == row)
        copies = [remote(src, dst, rseg_send.at[k, i], rseg_recv.at[k], (m, col)) for i, m in enumerate(row_mates)]
        keep = pltpu.make_async_copy(src, dst, local_sem.at[k])
        segments.append((inside, own, copies, keep))

        @pl.when(own)
        def _(copies=copies, keep=keep):
            for c in copies:
                c.start()
            keep.start()

    cm[...] = jnp.where(iota((cg, 8 * ch), 0) // GR == iota((cg, 8 * ch), 1) % ch, 1.0, 0.0).astype(BF)

    w2 = (0.5 * scale * dotf(wp[...], wh[...], ((1,), (1,)))).astype(BF)
    e_r = jnp.where(iota((cg, ch), 0) // GR == iota((cg, ch), 1), 1.0, 0.0).astype(BF)
    e_c = jnp.where(iota((heads, hg), 1) // GR == iota((heads, hg), 0), 1.0, 0.0).astype(BF)
    w2r = dotf(e_r, w2).astype(BF)
    same = iota((cg, hg), 0) % GR == iota((cg, hg), 1) % GR
    k2[...] = jnp.where(same, dotf(w2r, e_c), 0.0).astype(BF)

    jj, part = iota((2 * tc, 8 * ch), 0), iota((2 * tc, 8 * ch), 1)
    paired = jj // tc == part // (4 * ch)
    jj, part = jj % tc, part % (4 * ch) // ch
    drop = ((part == 0) & (jj < STEP) & col_first) | ((part == 2) & (jj >= tc - STEP) & col_last)
    es[0] = jnp.where(paired & ~drop & (part != 3), 1.0, 0.0).astype(BF)
    es[1] = jnp.where(paired & (part == 3), 1.0, 0.0).astype(BF)
    pr, ci = iota((4 * ch, cg), 0), iota((4 * ch, cg), 1)
    mine = (pr % ch == ci // GR) & (pr // ch < 3)
    top = (pr // ch == 0) & (ci % GR < STEP) & row_first
    low = (pr // ch == 2) & (ci % GR >= GR - STEP) & row_last
    ecol[0] = jnp.where(mine & ~top, 1.0, 0.0).astype(BF)
    ecol[1] = jnp.where(mine, 1.0, 0.0).astype(BF)
    ecol[2] = jnp.where(mine & ~low, 1.0, 0.0).astype(BF)
    ecx[...] = jnp.where(
        iota((4 * ch, hg), 0) == 3 * ch + iota((4 * ch, hg), 1) // GR, 1.0, 0.0).astype(BF)
    cs[...] = jnp.zeros_like(cs)
    lane_c = iota((1, 1, 8 * ch), 2) % ch
    loads[6].wait()

    def ahead(g, carry):
        start = pl.multiple_of(g * 2 * GR, 2 * GR)
        lanes = pl.ds(pl.multiple_of(g * 2 * tc, 256), 2 * tc)
        x = jnp.concatenate(
            [cot[:, pl.ds(start + k * GR, GR), :].reshape(hg, tc) for k in range(2)], axis=1)
        xs[:, lanes] = x
        ghs[:, lanes] = dotf(k2[...], x)
        y = dotf(x, es[1]).reshape(heads, GR, 8 * ch)
        y = jnp.sum(jnp.where(iota((heads, 1, 8 * ch), 0) == lane_c, y, 0.0), axis=0)
        rs[pl.ds(start, GR), :] = y[:, : 4 * ch]
        rs[pl.ds(start + GR, GR), :] = y[:, 4 * ch :]
        y = dotf(ecx[...], x)
        cs[...] += y[:, :tc] + y[:, tc:]
        return carry

    lax.fori_loop(0, groups // 2, ahead, 0)

    for inside, own, copies, keep in segments:

        @pl.when(own)
        def _(copies=copies, keep=keep):
            keep.wait()
            for c in copies:
                c.wait_send()

        @pl.when(inside & jnp.logical_not(own))
        def _(copies=copies):
            copies[0].wait_recv()

    @pl.when(row > 0)
    def _():
        up.wait_send()
        down.wait_recv()

    @pl.when(row < n_row - 1)
    def _():
        down.wait_send()
        up.wait_recv()

    lext[0:16, :] = lbuf[0, :, :ch].astype(F32)
    lext[16 : 16 + tr, :] = proj[:, :ch].astype(F32)
    lext[16 + tr :, :] = lbuf[1, :, :ch].astype(F32)
    rext[...] = rbuf[:, ch : 2 * ch].astype(F32)

    l_sh = [lext[16 + STEP * (a - 1) : 16 + STEP * (a - 1) + tr, :] for a in range(3)]
    r_sh = [rext[16 + STEP * (b - 1) : 16 + STEP * (b - 1) + tc, :] for b in range(3)]
    a1 = sum(l_sh[a] * (taps[a][0] + taps[a][1] + taps[a][2]) for a in range(3))
    da0 = sum(l_sh[a] * taps[a][0] for a in range(3))
    da2 = sum(l_sh[a] * taps[a][2] for a in range(3))
    da = -jnp.where(col_first, da0, jnp.where(col_last, da2, jnp.zeros_like(da2)))
    b1 = sum(r_sh[b] * (taps[0][b] + taps[1][b] + taps[2][b]) for b in range(3))
    db0 = sum(r_sh[b] * taps[0][b] for b in range(3))
    db2 = sum(r_sh[b] * taps[2][b] for b in range(3))
    db = -jnp.where(row_first, db0, jnp.where(row_last, db2, jnp.zeros_like(db2)))
    rind = jnp.where(edge(row_first, row_last, iota((tr, 2 * ch), 0), tr), 1.0, 0.0).astype(BF)
    qs[...] = jnp.concatenate(
        [*split(0.5 * a1), *split(0.5 * da), jnp.ones((tr, 2 * ch), BF), rind], axis=1)
    b_parts = [p.astype(F32) for p in (*split(0.5 * b1), *split(0.5 * db))]
    ns[4 * ch :, :] = jnp.concatenate(b_parts, axis=1).T.astype(BF)
    ns[: 2 * ch, :] = jnp.ones((2 * ch, tc), BF)
    ns[2 * ch : 4 * ch, :] = jnp.where(
        edge(col_first, col_last, iota((2 * ch, tc), 1), tc), 1.0, 0.0).astype(BF)

    chunk = 128
    n = chunk // GR

    def group(g, carry):
        start = pl.multiple_of(g * 2 * GR, 2 * GR)
        q = [qs[pl.ds(start + j * GR, GR), :] for j in range(2)]
        total = jnp.zeros((GR, 8 * ch), F32)
        for k in range(cg // chunk):
            rows = slice(k * chunk, (k + 1) * chunk)
            mask = cm[rows, :].reshape(n, GR, 8 * ch)
            for j in range(2):
                lanes = pl.ds(pl.multiple_of(g * 2 * tc + j * tc, 128), tc)
                u = dotf((mask * q[j][None]).reshape(chunk, 8 * ch), ns[...])
                t = jnp.tanh(u)
                p = 1.0 + t
                h = u * p
                hid[rows, lanes] = h.astype(BF)
                gcs[rows, j * tc : (j + 1) * tc] = (ghs[rows, lanes] * (p + h - h * t)).astype(BF)
            y = dotf(gcs[rows, :], es[0]).reshape(n, GR, 8 * ch)
            total = total + jnp.sum(jnp.where(iota((n, 1, 8 * ch), 0) + k * n == lane_c, y, 0.0), axis=0)
        rs[pl.ds(start, GR), :] += total[:, : 4 * ch]
        rs[pl.ds(start + GR, GR), :] += total[:, 4 * ch :]
        first = (g + groups - 1) // groups
        last = g // (groups // 2 - 1) + 1
        cs[...] += dotf(ecol[first], gcs[:, :tc]) + dotf(ecol[last], gcs[:, tc:])
        return carry

    lax.fori_loop(0, groups // 2, group, 0)

    cst = cs[...].T
    rsv = rs[...]
    eye = iota((ch, ch), 0) == iota((ch, ch), 1)
    whs = scale * jnp.concatenate([wh[...].astype(F32), jnp.zeros((ch - heads, ch), F32)], axis=0)
    zc = jnp.zeros((ch, ch), F32)

    def spread(tap):
        blocks = [[jnp.where(eye, tap(n, m), 0.0) for m in range(3)] + [zc] for n in range(3)]
        blocks.append([zc, zc, zc, whs])
        return jnp.concatenate([jnp.concatenate(b, axis=1) for b in blocks], axis=0)

    for sums, z, out, length, weights in (
        (rsv, zl, plx, tr, spread(lambda b, a: taps[a][b])),
        (cst, zr, prx, tc, spread(lambda a, b: taps[a][b])),
    ):
        z[:16, :] = jnp.zeros((16, 4 * ch), F32)
        z[16 + length :, :] = jnp.zeros((16, 4 * ch), F32)
        z[16 : 16 + length, :] = dotf(sums, weights, precision=HI)
        ext = z[8 : 24 + length, 3 * ch :]
        for n in range(3):
            ext = ext + z[12 - STEP * n : 28 - STEP * n + length, n * ch : (n + 1) * ch]
        out[...] = ext

    lanes = 4 * ch
    pp, sp = tr // 4 // n_col, 2 * ch // n_col
    colsend[...] = pack(plx[8 : 8 + tr, :]).reshape(n_col, pp, lanes)
    pad = jnp.zeros((8, 3 * ch), F32)
    halosend[0] = jnp.concatenate([plx[:8, :], pad], axis=1)
    halosend[1] = jnp.concatenate([plx[8 + tr :, :], pad], axis=1)
    pr = (tc + 16) // 4
    rowsend[...] = pack(prx[...])

    def to_col(src, dst, send, recv):
        return [remote(src(m), dst.at[col], send.at[m], recv.at[col], (row, m)) for m in col_mates]

    def to_row(src, dst, send, recv):
        return [remote(src, dst.at[row], send.at[m], recv.at[row], (m, col)) for m in row_mates]

    def from_col(src, dst, send, recv):
        return [remote(src(m), dst.at[m], send.at[m], recv.at[m], (row, m)) for m in col_mates]

    def from_row(src, dst, send, recv):
        return [remote(src, dst.at[m], send.at[m], recv.at[m], (m, col)) for m in row_mates]

    def start(copies):
        for c in copies:
            c.start()

    def arrived(copies):
        for c in copies:
            c.wait_recv()

    def sent(copies):
        for c in copies:
            c.wait_send()

    hup = remote(halosend.at[0], halorecv.at[1], h1s.at[0], h1r.at[1], (row - 1, col))
    hdown = remote(halosend.at[1], halorecv.at[0], h1s.at[1], h1r.at[0], (row + 1, col))
    p1c = (lambda m: colsend.at[m], colrecv, c1s, c1r)
    p1r = (rowsend, rowrecv, r1s, r1r)
    s1c, s1r = to_col(*p1c), to_row(*p1r)
    start(s1c)
    start(s1r)
    pl.when(row > 0)(hup.start)
    pl.when(row < n_row - 1)(hdown.start)
    prod = dotf(hid[...], xs[...], ((1,), (1,)))
    prod = jnp.sum(jnp.where(same, prod, 0.0).reshape(ch, GR, hg), axis=1)
    e_h = jnp.where(iota((hg, ch), 0) // GR == iota((hg, ch), 1), 1.0, 0.0)
    hc = dotf(prod, e_h, precision=HI)
    pc = dotf(l_sh[1], rsv[:, 3 * ch :], ((0,), (0,)), HI) + dotf(r_sh[1], cst[:, 3 * ch :], ((0,), (0,)), HI)
    small[:ch, :] = jnp.concatenate([hc, pc, jnp.zeros((ch, 2 * ch), F32)], axis=1)
    rows_out = []
    zero_l, zero_r = jnp.zeros((tr, ch), F32), jnp.zeros((tc, ch), F32)
    for a in range(3):
        rows_out.append(jnp.sum(jnp.concatenate([l_sh[a]] * 3 + [zero_l], axis=1) * rsv, axis=0, keepdims=True))
    for b in range(3):
        rows_out.append(jnp.sum(jnp.concatenate([r_sh[b]] * 3 + [zero_r], axis=1) * cst, axis=0, keepdims=True))
    small[ch : ch + 8, :] = jnp.concatenate(rows_out + [jnp.zeros((2, 4 * ch), F32)], axis=0)
    small[ch + 8 :, :] = jnp.zeros((ch - 8, 4 * ch), F32)
    smsend[...] = small[...].reshape(n_col, sp, lanes)
    p1s = (lambda m: smsend.at[m], smrecv, m1s, m1r)
    s1s = to_col(*p1s)
    start(s1s)
    arrived(from_col(*p1c))
    piece = colsend[col]
    for m in col_mates:
        piece = piece + colrecv[m]
    arrived(from_row(*p1r))
    right = rowsend[...]
    for m in row_mates:
        right = right + rowrecv[m]

    @pl.when(row > 0)
    def _():
        hup.wait_send()
        hdown.wait_recv()

    @pl.when(row < n_row - 1)
    def _():
        hdown.wait_send()
        hup.wait_recv()

    fill = [jnp.zeros((agsend.shape[0] - pp - 4 - pr, lanes), F32)] if agsend.shape[0] > pp + 4 + pr else []
    agsend[...] = jnp.concatenate(
        [right, pack(halorecv[0, :, :ch]), pack(halorecv[1, :, :ch]), piece] + fill, axis=0).astype(BF)
    p2c = (lambda m: agsend, agrecv, c2s, c2r)
    s2c = to_col(*p2c)
    start(s2c)
    arrived(from_col(*p1s))
    part = smsend[col]
    for m in col_mates:
        part = part + smrecv[m]
    spsend[...] = part
    p2r = (spsend, sprecv, r2s, r2r)
    s2r = to_row(*p2r)
    start(s2r)
    sent(s1c)
    sent(s1r)
    sent(s1s)
    arrived(from_col(*p2c))
    sent(s2c)
    agrecv[col] = agsend[...]
    gl = unpack(jnp.concatenate([agrecv[m, pr + 4 : pr + 4 + pp, :].astype(F32) for m in range(n_col)], axis=0))
    halo = sum(agrecv[m, pr : pr + 4, :].astype(F32) for m in range(n_col))
    gl = jnp.concatenate([gl[:8] + unpack(halo[:2]), gl[8:-8], gl[-8:] + unpack(halo[2:])], axis=0)
    window[...] = jnp.zeros_like(window)
    for k in range(tr // tc + 2):
        m = lax.div(row * tr, tc) - 1 + k

        @pl.when((m >= 0) & (m < n_col))
        def _(m=m, k=k):
            window[k * tc : k * tc + tc + 16, :] += unpack(agrecv[m, :pr, :].astype(F32))

    gr = window[tc + 8 : tc + 8 + tr, :]
    glb, grb = gl.astype(BF), gr.astype(BF)
    both = jnp.concatenate([gl, gr, jnp.zeros((tr, 2 * ch), F32)], axis=1).T[: 2 * ch].astype(BF)
    part = scale * dotf(both, feats[...])

    gwsend[...] = part.astype(BF)
    p3r = (gwsend, gwrecv, r3s, r3r)
    s3r = to_row(*p3r)
    start(s3r)
    arrived(from_row(*p2r))
    total = spsend[...]
    for m in row_mates:
        total = total + sprecv[m]
    sfin[col] = total
    p3c = (lambda m: sfin.at[col], sfin, c3s, c3r)
    s3c = to_col(*p3c)
    start(s3c)
    gf_out[...] = (dotf(glb, wl[...]) + dotf(grb, wr[...])).astype(BF)
    arrived(from_col(*p3c))
    sent(s3c)
    sent(s2r)
    full = jnp.concatenate([sfin[m] for m in range(n_col)], axis=0)
    hc, pc = full[:ch, :heads], full[:ch, ch : ch + heads]
    for a in range(3):
        for b in range(3):
            gk_out[3 * a + b : 3 * a + b + 1, :] = scale * (
                full[ch + a : ch + a + 1, b * ch : (b + 1) * ch]
                + full[ch + 3 + b : ch + 4 + b, a * ch : (a + 1) * ch])
    gp_out[...] = scale * scale * dotf(hc, wh[...].astype(F32), precision=HI)
    gh_out[...] = (scale * (pc + dotf(wp[...].astype(F32), hc, ((0,), (0,)), HI))).T
    arrived(from_row(*p3r))
    for m in row_mates:
        part = part + gwrecv[m].astype(F32)
    gwl_out[...] = part[:ch]
    gwr_out[...] = part[ch:]
    sent(s3r)


def move_kernel(*refs):
    sems = refs[-1]
    n = len(refs) // 2
    copies = [pltpu.make_async_copy(refs[k], refs[n + k], sems.at[k]) for k in range(n)]
    for c in copies:
        c.start()
    for c in copies:
        c.wait()


def body(bin_features, w_left, w_right, depth_kernel, w_point, w_head, cotangent):
    ch, heads = w_head.shape
    tr, tc = cotangent.shape[1:]
    n_row, n_col = lax.axis_size("row"), lax.axis_size("col")
    scale = 1.0 / math.sqrt(tr * n_row)
    cg, hg, groups = ch * GR, heads * GR, tr // GR
    d, lanes = w_left.shape[0], 4 * ch
    pp, sp, pr = tr // 4 // n_col, 2 * ch // n_col, (tc + 16) // 4
    ag = -(-(pp + 4 + pr) // 16) * 16
    vm = pl.BlockSpec(memory_space=pltpu.VMEM)
    dma = pltpu.SemaphoreType.DMA
    operands = (bin_features, w_left.T, w_right.T, depth_kernel, w_point, w_head.T, cotangent)
    outs = pl.pallas_call(
        functools.partial(tile_kernel, scale),
        out_shape=(
            pltpu.VMEM((tr, d), BF),
            pltpu.VMEM((ch, d), F32),
            pltpu.VMEM((ch, d), F32),
            pltpu.VMEM((9, ch), F32),
            pltpu.VMEM((ch, ch), F32),
            pltpu.VMEM((heads, ch), F32),
        ),
        in_specs=[pl.BlockSpec(memory_space=pltpu.HBM)] * 7,
        out_specs=(vm,) * 6,
        scratch_shapes=[
            *(pltpu.VMEM(v.shape, v.dtype) for v in operands),
            dma((7,)),
            pltpu.VMEM((cg, groups * tc), F32),
            pltpu.VMEM((tr + 32, ch), F32),
            pltpu.VMEM((tc + 32, ch), F32),
            pltpu.VMEM((tr + 16, ch), F32),
            pltpu.VMEM((tc + 16, ch), F32),
            pltpu.VMEM((2 * ch, lanes), F32),
            pltpu.VMEM((tr, 8 * ch), BF),
            pltpu.VMEM((8 * ch, tc), BF),
            pltpu.VMEM((cg, hg), BF),
            pltpu.VMEM((cg, 8 * ch), BF),
            pltpu.VMEM((2, 2 * tc, 8 * ch), BF),
            pltpu.VMEM((3, 4 * ch, cg), BF),
            pltpu.VMEM((4 * ch, hg), BF),
            pltpu.VMEM((tr, 4 * ch), F32),
            pltpu.VMEM((4 * ch, tc), F32),
            pltpu.VMEM((cg, 2 * tc), BF),
            pltpu.VMEM((cg, groups * tc), BF),
            pltpu.VMEM((hg, groups * tc), BF),
            pltpu.VMEM((tr + 32, 4 * ch), F32),
            pltpu.VMEM((tc + 32, 4 * ch), F32),
            pltpu.VMEM((tr, lanes), BF),
            pltpu.VMEM((2, 16, lanes), BF),
            pltpu.VMEM((tc + 32, lanes), BF),
            pltpu.VMEM((n_col, pp, lanes), F32),
            pltpu.VMEM((n_col, pp, lanes), F32),
            pltpu.VMEM((pr, lanes), F32),
            pltpu.VMEM((n_row, pr, lanes), F32),
            pltpu.VMEM((2, 8, lanes), F32),
            pltpu.VMEM((2, 8, lanes), F32),
            pltpu.VMEM((n_col, sp, lanes), F32),
            pltpu.VMEM((n_col, sp, lanes), F32),
            dma((n_col,)), dma((n_col,)),
            pltpu.VMEM((ag, lanes), BF),
            pltpu.VMEM((n_col, ag, lanes), BF),
            pltpu.VMEM((sp, lanes), F32),
            pltpu.VMEM((n_row, sp, lanes), F32),
            pltpu.VMEM((n_col, sp, lanes), F32),
            pltpu.VMEM((2 * ch, d), BF),
            pltpu.VMEM((n_row, 2 * ch, d), BF),
            pltpu.VMEM((tr + 2 * tc + 16, ch), F32),
            dma((3, n_row)), dma((3,)), dma((2,)), dma((2,)),
            dma((n_col,)), dma((n_col,)), dma((n_row,)), dma((n_row,)), dma((2,)), dma((2,)),
            dma((n_col,)), dma((n_col,)), dma((n_row,)), dma((n_row,)),
            dma((n_col,)), dma((n_col,)), dma((n_row,)), dma((n_row,)),
            dma((3,)),
        ],
        compiler_params=pltpu.CompilerParams(
            vmem_limit_bytes=63 * 1024 * 1024, collective_id=0, has_side_effects=True),
    )(*operands)
    hbm = pl.BlockSpec(memory_space=pltpu.HBM)
    gf, gwl, gwr, gk, gp, gh = pl.pallas_call(
        move_kernel,
        out_shape=tuple(jax.ShapeDtypeStruct(v.shape, v.dtype) for v in outs),
        in_specs=[vm] * 6,
        out_specs=(hbm,) * 6,
        scratch_shapes=[dma((6,))],
        compiler_params=pltpu.CompilerParams(vmem_limit_bytes=16 * 1024 * 1024),
    )(*outs)
    return gf, gwl.T, gwr.T, gk, gp, gh.T


def solution(mesh):
    return jax.shard_map(
        body,
        mesh=mesh,
        in_specs=(P("row", None), P(), P(), P(), P(), P(), P(None, "row", "col")),
        out_specs=(P("row", None), P(), P(), P(), P(), P()),
        check_vma=False,
    )
```

```python
import functools
import math

import jax
import jax.numpy as jnp
from jax import lax
from jax.experimental import pallas as pl
from jax.experimental.pallas import tpu as pltpu
from jax.sharding import PartitionSpec as P

STEP = 4
BF = jnp.bfloat16
F32 = jnp.float32
HI = lax.Precision.HIGHEST
GR = 16


def iota(shape, dim):
    return lax.broadcasted_iota(jnp.int32, shape, dim)


def split(x):
    hi = x.astype(BF)
    return hi, (x - hi.astype(F32)).astype(BF)


def dotf(a, b, contract=((1,), (0,)), precision=None):
    return lax.dot_general(a, b, (contract, ((), ())), precision=precision, preferred_element_type=F32)


MESH = pl.DeviceIdType.MESH


def pack(x):
    n = x.shape[0] // 4
    return jnp.concatenate([x[k * n : (k + 1) * n] for k in range(4)], axis=1)


def unpack(x):
    n = x.shape[1] // 4
    return jnp.concatenate([x[:, k * n : (k + 1) * n] for k in range(4)], axis=0)


def tile_kernel(scale, feats_hbm, wl_hbm, wr_hbm, dk_hbm, wp_hbm, wh_hbm, cot_hbm,
                gf_out, gwl_out, gwr_out, gk_out, gp_out, gh_out,
                feats, wl, wr, dk, wp, wh, cot, load_sem, ghs,
                lext, rext, plx, prx, small, qs, ns, k2, cm, es, ecol, colsum, us, fall, fsend, frecv, rs, cs, gcs, hid, xs, zl, zr,
                proj, lbuf, rbuf, colsend, colrecv, rowsend, rowrecv, halosend, halorecv,
                smsend, smrecv, m1s, m1r,
                agsend, agrecv, spsend, sprecv, sfin, gwsend, gwrecv, window,
                rseg_send, rseg_recv, lseg_send, lseg_recv, c1s, c1r, r1s, r1r, h1s, h1r,
                c2s, c2r, r2s, r2r, c3s, c3r, r3s, r3r, local_sem):
    loads = [pltpu.make_async_copy(src, dst, load_sem.at[k]) for k, (src, dst) in enumerate((
        (feats_hbm, feats), (wl_hbm, wl), (wr_hbm, wr), (dk_hbm, dk), (wp_hbm, wp), (wh_hbm, wh), (cot_hbm, cot)))]
    for copy in loads:
        copy.start()
    heads, ch = wh.shape
    tr, tc = cot.shape[1:]
    groups = tr // GR
    cg, hg = ch * GR, heads * GR
    row, col = lax.axis_index("row"), lax.axis_index("col")
    row_first, row_last = row == 0, row == lax.axis_size("row") - 1
    col_first, col_last = col == 0, col == lax.axis_size("col") - 1
    def edge(first, last, pos, length):
        return ((pos < STEP) & first) | ((pos >= length - STEP) & last)

    n_row, n_col = lax.axis_size("row"), lax.axis_size("col")
    nb = tr * n_row
    row_mates = [lax.rem(row + k, n_row) for k in range(1, n_row)]
    col_mates = [lax.rem(col + k, n_col) for k in range(1, n_col)]

    lbuf[...] = jnp.zeros_like(lbuf)
    halorecv[...] = jnp.zeros_like(halorecv)
    for first, count in ((0, 16), (16 + tc, 16)):
        rbuf[first : first + count, :] = jnp.zeros((count, 4 * ch), BF)
    barrier = pltpu.get_barrier_semaphore()
    for m in row_mates:
        pl.semaphore_signal(barrier, inc=1, device_id=(m, col), device_id_type=MESH)
    for m in col_mates:
        pl.semaphore_signal(barrier, inc=1, device_id=(row, m), device_id_type=MESH)

    for copy in loads[:6]:
        copy.wait()
    taps = [[dk[3 * a + b : 3 * a + b + 1, :] for b in range(3)] for a in range(3)]

    weights = jnp.concatenate([wl[...], wr[...], jnp.zeros((2 * ch, wl.shape[1]), BF)], axis=0)
    proj[...] = dotf(feats[...], weights, ((1,), (1,))).astype(BF)
    pl.semaphore_wait(barrier, n_row + n_col - 2)

    def remote(src, dst, send, recv, device):
        return pltpu.make_async_remote_copy(
            src_ref=src, dst_ref=dst, send_sem=send, recv_sem=recv, device_id=device, device_id_type=MESH)

    up = remote(proj.at[pl.ds(0, 16)], lbuf.at[1], lseg_send.at[0], lseg_recv.at[1], (row - 1, col))
    down = remote(proj.at[pl.ds(tr - 16, 16)], lbuf.at[0], lseg_send.at[1], lseg_recv.at[0], (row + 1, col))
    pl.when(row > 0)(up.start)
    pl.when(row < n_row - 1)(down.start)
    segments = []
    for k, (offset, first, count) in enumerate(((-16, 0, 16), (0, 16, tc), (tc, 16 + tc, 16))):
        bin0 = col * tc + offset
        inside = (bin0 >= 0) & (bin0 < nb)
        owner = lax.div(bin0 + nb, tr) - n_row
        local = pl.multiple_of(lax.rem(bin0 + nb, tr), 16)
        src = proj.at[pl.ds(local, count)]
        dst = rbuf.at[pl.ds(first, count)]
        own = inside & (owner == row)
        copies = [remote(src, dst, rseg_send.at[k, i], rseg_recv.at[k], (m, col)) for i, m in enumerate(row_mates)]
        keep = pltpu.make_async_copy(src, dst, local_sem.at[k])
        segments.append((inside, own, copies, keep))

        @pl.when(own)
        def _(copies=copies, keep=keep):
            for c in copies:
                c.start()
            keep.start()

    cm[...] = jnp.where(iota((cg, 8 * ch), 0) // GR == iota((cg, 8 * ch), 1) % ch, 1.0, 0.0).astype(BF)

    w2 = (0.5 * scale * dotf(wp[...], wh[...], ((1,), (1,)))).astype(BF)
    e_r = jnp.where(iota((cg, ch), 0) // GR == iota((cg, ch), 1), 1.0, 0.0).astype(BF)
    e_c = jnp.where(iota((heads, hg), 1) // GR == iota((heads, hg), 0), 1.0, 0.0).astype(BF)
    w2r = dotf(e_r, w2).astype(BF)
    same = iota((cg, hg), 0) % GR == iota((cg, hg), 1) % GR
    k2[:cg, :] = jnp.where(same, dotf(w2r, e_c), 0.0).astype(BF)
    k2[cg:, :] = jnp.where(iota((ch, hg), 0) == iota((ch, hg), 1) // GR, 1.0, 0.0).astype(BF)

    jj, part = iota((2 * tc, 8 * ch), 0), iota((2 * tc, 8 * ch), 1)
    paired = jj // tc == part // (4 * ch)
    jj, part = jj % tc, part % (4 * ch) // ch
    drop = ((part == 0) & (jj < STEP) & col_first) | ((part == 2) & (jj >= tc - STEP) & col_last)
    es[0] = jnp.where(paired & ~drop & (part != 3), 1.0, 0.0).astype(BF)
    es[1] = jnp.where(paired & (part == 3), 1.0, 0.0).astype(BF)
    pr, ci = iota((ch, cg), 0), iota((ch, cg), 1)
    mine = pr == ci // GR
    ecol[0] = jnp.where(mine & (ci % GR < STEP) & row_first, 1.0, 0.0).astype(BF)
    ecol[1] = jnp.where(mine & (ci % GR >= GR - STEP) & row_last, 1.0, 0.0).astype(BF)
    colsum[...] = jnp.zeros_like(colsum)
    fs = [remote(feats, fall.at[row], fsend.at[m], frecv.at[row], (m, col)) for m in row_mates]
    fr = [remote(feats, fall.at[m], fsend.at[m], frecv.at[m], (m, col)) for m in row_mates]
    cs[...] = jnp.zeros_like(cs)
    lane_c = iota((1, 1, 8 * ch), 2) % ch
    loads[6].wait()

    def ahead(g, carry):
        start = pl.multiple_of(g * 2 * GR, 2 * GR)
        lanes = pl.ds(pl.multiple_of(g * 2 * tc, 256), 2 * tc)
        x = jnp.concatenate(
            [cot[:, pl.ds(start + k * GR, GR), :].reshape(hg, tc) for k in range(2)], axis=1)
        xs[:, lanes] = x
        w = dotf(k2[...], x)
        ghs[:, lanes] = w[:cg]
        cs[...] += w[cg:, :tc] + w[cg:, tc:]
        y = dotf(x, es[1]).reshape(heads, GR, 8 * ch)
        y = jnp.sum(jnp.where(iota((heads, 1, 8 * ch), 0) == lane_c, y, 0.0), axis=0)
        rs[pl.ds(start, GR), :] = y[:, : 4 * ch]
        rs[pl.ds(start + GR, GR), :] = y[:, 4 * ch :]
        return carry

    lax.fori_loop(0, groups // 2, ahead, 0)

    for inside, own, copies, keep in segments:

        @pl.when(own)
        def _(copies=copies, keep=keep):
            keep.wait()
            for c in copies:
                c.wait_send()

        @pl.when(inside & jnp.logical_not(own))
        def _(copies=copies):
            copies[0].wait_recv()

    @pl.when(row > 0)
    def _():
        up.wait_send()
        down.wait_recv()

    @pl.when(row < n_row - 1)
    def _():
        down.wait_send()
        up.wait_recv()

    for copy in fs:
        copy.start()
    lext[0:16, :] = lbuf[0, :, :ch].astype(F32)
    lext[16 : 16 + tr, :] = proj[:, :ch].astype(F32)
    lext[16 + tr :, :] = lbuf[1, :, :ch].astype(F32)
    rext[...] = rbuf[:, ch : 2 * ch].astype(F32)

    l_sh = [lext[16 + STEP * (a - 1) : 16 + STEP * (a - 1) + tr, :] for a in range(3)]
    r_sh = [rext[16 + STEP * (b - 1) : 16 + STEP * (b - 1) + tc, :] for b in range(3)]
    a1 = sum(l_sh[a] * (taps[a][0] + taps[a][1] + taps[a][2]) for a in range(3))
    da0 = sum(l_sh[a] * taps[a][0] for a in range(3))
    da2 = sum(l_sh[a] * taps[a][2] for a in range(3))
    da = -jnp.where(col_first, da0, jnp.where(col_last, da2, jnp.zeros_like(da2)))
    b1 = sum(r_sh[b] * (taps[0][b] + taps[1][b] + taps[2][b]) for b in range(3))
    db0 = sum(r_sh[b] * taps[0][b] for b in range(3))
    db2 = sum(r_sh[b] * taps[2][b] for b in range(3))
    db = -jnp.where(row_first, db0, jnp.where(row_last, db2, jnp.zeros_like(db2)))
    rind = jnp.where(edge(row_first, row_last, iota((tr, 2 * ch), 0), tr), 1.0, 0.0).astype(BF)
    qs[...] = jnp.concatenate(
        [*split(0.5 * a1), *split(0.5 * da), jnp.ones((tr, 2 * ch), BF), rind], axis=1)
    b_parts = [p.astype(F32) for p in (*split(0.5 * b1), *split(0.5 * db))]
    ns[4 * ch :, :] = jnp.concatenate(b_parts, axis=1).T.astype(BF)
    ns[: 2 * ch, :] = jnp.ones((2 * ch, tc), BF)
    ns[2 * ch : 4 * ch, :] = jnp.where(
        edge(col_first, col_last, iota((2 * ch, tc), 1), tc), 1.0, 0.0).astype(BF)

    chunk = 64
    n = chunk // GR

    def pair(g, slot):
        start = pl.multiple_of(g * 2 * GR, 2 * GR)
        mask = cm[...].reshape(ch, GR, 8 * ch)
        for j in range(2):
            q = qs[pl.ds(start + j * GR, GR), :]
            us[slot, :, j * tc : (j + 1) * tc] = dotf((mask * q[None]).reshape(cg, 8 * ch), ns[...])
        lanes = pl.ds(pl.multiple_of(g * 2 * tc, 256), 2 * tc)
        for k in range(cg // chunk):
            rows = slice(k * chunk, (k + 1) * chunk)
            u = us[slot, rows, :]
            t = jnp.tanh(u)
            p = 1.0 + t
            h = u * p
            hid[rows, lanes] = h.astype(BF)
            gc = ghs[rows, lanes] * (p + h - h * t)
            gcs[rows, lanes] = gc.astype(BF)
            colsum[k * n : (k + 1) * n] += jnp.sum(gc.reshape(n, 2, 8, 2 * tc), axis=1)
        y = dotf(gcs[:, lanes], es[0]).reshape(ch, GR, 8 * ch)
        total = jnp.sum(jnp.where(iota((ch, 1, 8 * ch), 0) == lane_c, y, 0.0), axis=0)
        rs[pl.ds(start, GR), :] += total[:, : 4 * ch]
        rs[pl.ds(start + GR, GR), :] += total[:, 4 * ch :]

    def group(g, carry):
        pair(2 * g, 0)
        pair(2 * g + 1, 1)
        return carry

    lax.fori_loop(0, groups // 4, group, 0)
    base = jnp.sum(colsum[...], axis=1)
    base = base[:, :tc] + base[:, tc:]
    top = dotf(ecol[0], gcs[:, :tc])
    low = dotf(ecol[1], gcs[:, (groups - 1) * tc :])
    cst = jnp.concatenate([base - top, base, base - low, cs[...]], axis=0).T
    rsv = rs[...]
    eye = iota((ch, ch), 0) == iota((ch, ch), 1)
    whs = scale * jnp.concatenate([wh[...].astype(F32), jnp.zeros((ch - heads, ch), F32)], axis=0)
    zc = jnp.zeros((ch, ch), F32)

    def spread(tap):
        blocks = [[jnp.where(eye, tap(n, m), 0.0) for m in range(3)] + [zc] for n in range(3)]
        blocks.append([zc, zc, zc, whs])
        return jnp.concatenate([jnp.concatenate(b, axis=1) for b in blocks], axis=0)

    for sums, z, out, length, weights in (
        (rsv, zl, plx, tr, spread(lambda b, a: taps[a][b])),
        (cst, zr, prx, tc, spread(lambda a, b: taps[a][b])),
    ):
        z[:16, :] = jnp.zeros((16, 4 * ch), F32)
        z[16 + length :, :] = jnp.zeros((16, 4 * ch), F32)
        z[16 : 16 + length, :] = dotf(sums, weights, precision=HI)
        ext = z[8 : 24 + length, 3 * ch :]
        for n in range(3):
            ext = ext + z[12 - STEP * n : 28 - STEP * n + length, n * ch : (n + 1) * ch]
        out[...] = ext

    lanes = 4 * ch
    pp, sp = tr // 4 // n_col, 2 * ch // n_col
    colsend[...] = pack(plx[8 : 8 + tr, :]).reshape(n_col, pp, lanes)
    pad = jnp.zeros((8, 3 * ch), F32)
    halosend[0] = jnp.concatenate([plx[:8, :], pad], axis=1)
    halosend[1] = jnp.concatenate([plx[8 + tr :, :], pad], axis=1)
    pr = (tc + 16) // 4
    rowsend[...] = pack(prx[...])

    def to_col(src, dst, send, recv):
        return [remote(src(m), dst.at[col], send.at[m], recv.at[col], (row, m)) for m in col_mates]

    def to_row(src, dst, send, recv):
        return [remote(src, dst.at[row], send.at[m], recv.at[row], (m, col)) for m in row_mates]

    def from_col(src, dst, send, recv):
        return [remote(src(m), dst.at[m], send.at[m], recv.at[m], (row, m)) for m in col_mates]

    def from_row(src, dst, send, recv):
        return [remote(src, dst.at[m], send.at[m], recv.at[m], (m, col)) for m in row_mates]

    def start(copies):
        for c in copies:
            c.start()

    def arrived(copies):
        for c in copies:
            c.wait_recv()

    def sent(copies):
        for c in copies:
            c.wait_send()

    hup = remote(halosend.at[0], halorecv.at[1], h1s.at[0], h1r.at[1], (row - 1, col))
    hdown = remote(halosend.at[1], halorecv.at[0], h1s.at[1], h1r.at[0], (row + 1, col))
    p1c = (lambda m: colsend.at[m], colrecv, c1s, c1r)
    p1r = (rowsend, rowrecv, r1s, r1r)
    s1c, s1r = to_col(*p1c), to_row(*p1r)
    start(s1c)
    start(s1r)
    pl.when(row > 0)(hup.start)
    pl.when(row < n_row - 1)(hdown.start)
    prod = dotf(hid[...], xs[...], ((1,), (1,)))
    prod = jnp.sum(jnp.where(same, prod, 0.0).reshape(ch, GR, hg), axis=1)
    e_h = jnp.where(iota((hg, ch), 0) // GR == iota((hg, ch), 1), 1.0, 0.0)
    hc = dotf(prod, e_h, precision=HI)
    pc = dotf(l_sh[1], rsv[:, 3 * ch :], ((0,), (0,)), HI) + dotf(r_sh[1], cst[:, 3 * ch :], ((0,), (0,)), HI)
    small[:ch, :] = jnp.concatenate([hc, pc, jnp.zeros((ch, 2 * ch), F32)], axis=1)
    rows_out = []
    zero_l, zero_r = jnp.zeros((tr, ch), F32), jnp.zeros((tc, ch), F32)
    for a in range(3):
        rows_out.append(jnp.sum(jnp.concatenate([l_sh[a]] * 3 + [zero_l], axis=1) * rsv, axis=0, keepdims=True))
    for b in range(3):
        rows_out.append(jnp.sum(jnp.concatenate([r_sh[b]] * 3 + [zero_r], axis=1) * cst, axis=0, keepdims=True))
    small[ch : ch + 8, :] = jnp.concatenate(rows_out + [jnp.zeros((2, 4 * ch), F32)], axis=0)
    small[ch + 8 :, :] = jnp.zeros((ch - 8, 4 * ch), F32)
    smsend[...] = small[...].reshape(n_col, sp, lanes)
    p1s = (lambda m: smsend.at[m], smrecv, m1s, m1r)
    s1s = to_col(*p1s)
    start(s1s)
    arrived(from_col(*p1c))
    piece = colsend[col]
    for m in col_mates:
        piece = piece + colrecv[m]
    arrived(from_row(*p1r))
    right = rowsend[...]
    for m in row_mates:
        right = right + rowrecv[m]

    @pl.when(row > 0)
    def _():
        hup.wait_send()
        hdown.wait_recv()

    @pl.when(row < n_row - 1)
    def _():
        hdown.wait_send()
        hup.wait_recv()

    fill = [jnp.zeros((agsend.shape[0] - pp - 4 - pr, lanes), F32)] if agsend.shape[0] > pp + 4 + pr else []
    agsend[...] = jnp.concatenate(
        [right, pack(halorecv[0, :, :ch]), pack(halorecv[1, :, :ch]), piece] + fill, axis=0).astype(BF)
    p2c = (lambda m: agsend, agrecv, c2s, c2r)
    s2c = to_col(*p2c)
    start(s2c)
    arrived(from_col(*p1s))
    part = smsend[col]
    for m in col_mates:
        part = part + smrecv[m]
    spsend[...] = part
    p2r = (spsend, sprecv, r2s, r2r)
    s2r = to_row(*p2r)
    start(s2r)
    sent(s1c)
    sent(s1r)
    sent(s1s)
    arrived(from_col(*p2c))
    sent(s2c)
    agrecv[col] = agsend[...]
    gl = unpack(jnp.concatenate([agrecv[m, pr + 4 : pr + 4 + pp, :].astype(F32) for m in range(n_col)], axis=0))
    halo = sum(agrecv[m, pr : pr + 4, :].astype(F32) for m in range(n_col))
    gl = jnp.concatenate([gl[:8] + unpack(halo[:2]), gl[8:-8], gl[-8:] + unpack(halo[2:])], axis=0)
    window[...] = jnp.zeros_like(window)
    for k in range(tr // tc + 2):
        m = lax.div(row * tr, tc) - 1 + k

        @pl.when((m >= 0) & (m < n_col))
        def _(m=m, k=k):
            window[k * tc : k * tc + tc + 16, :] += unpack(agrecv[m, :pr, :].astype(F32))

    gr = window[tc + 8 : tc + 8 + tr, :]
    glb, grb = gl.astype(BF), gr.astype(BF)
    both = jnp.concatenate([gl, gr, jnp.zeros((tr, 2 * ch), F32)], axis=1).T[: 2 * ch].astype(BF)

    gwsend[...] = both
    p3r = (gwsend, gwrecv, r3s, r3r)
    s3r = to_row(*p3r)
    start(s3r)
    part = dotf(both, feats[...])
    arrived(from_row(*p2r))
    total = spsend[...]
    for m in row_mates:
        total = total + sprecv[m]
    sfin[col] = total
    p3c = (lambda m: sfin.at[col], sfin, c3s, c3r)
    s3c = to_col(*p3c)
    start(s3c)
    gf_out[...] = (dotf(glb, wl[...]) + dotf(grb, wr[...])).astype(BF)
    arrived(from_col(*p3c))
    sent(s3c)
    sent(s2r)
    full = jnp.concatenate([sfin[m] for m in range(n_col)], axis=0)
    hc, pc = full[:ch, :heads], full[:ch, ch : ch + heads]
    for a in range(3):
        for b in range(3):
            gk_out[3 * a + b : 3 * a + b + 1, :] = scale * (
                full[ch + a : ch + a + 1, b * ch : (b + 1) * ch]
                + full[ch + 3 + b : ch + 4 + b, a * ch : (a + 1) * ch])
    gp_out[...] = scale * scale * dotf(hc, wh[...].astype(F32), precision=HI)
    gh_out[...] = (scale * (pc + dotf(wp[...].astype(F32), hc, ((0,), (0,)), HI))).T
    arrived(from_row(*p3r))
    arrived(fr)
    for m in row_mates:
        part = part + dotf(gwrecv[m], fall[m])
    part = scale * part
    sent(fs)
    gwl_out[...] = part[:ch]
    gwr_out[...] = part[ch:]
    sent(s3r)


def move_kernel(*refs):
    sems = refs[-1]
    n = len(refs) // 2
    copies = [pltpu.make_async_copy(refs[k], refs[n + k], sems.at[k]) for k in range(n)]
    for c in copies:
        c.start()
    for c in copies:
        c.wait()


def body(bin_features, w_left, w_right, depth_kernel, w_point, w_head, cotangent):
    ch, heads = w_head.shape
    tr, tc = cotangent.shape[1:]
    n_row, n_col = lax.axis_size("row"), lax.axis_size("col")
    scale = 1.0 / math.sqrt(tr * n_row)
    cg, hg, groups = ch * GR, heads * GR, tr // GR
    d, lanes = w_left.shape[0], 4 * ch
    pp, sp, pr = tr // 4 // n_col, 2 * ch // n_col, (tc + 16) // 4
    ag = -(-(pp + 4 + pr) // 16) * 16
    vm = pl.BlockSpec(memory_space=pltpu.VMEM)
    dma = pltpu.SemaphoreType.DMA
    operands = (bin_features, w_left.T, w_right.T, depth_kernel, w_point, w_head.T, cotangent)
    outs = pl.pallas_call(
        functools.partial(tile_kernel, scale),
        out_shape=(
            pltpu.VMEM((tr, d), BF),
            pltpu.VMEM((ch, d), F32),
            pltpu.VMEM((ch, d), F32),
            pltpu.VMEM((9, ch), F32),
            pltpu.VMEM((ch, ch), F32),
            pltpu.VMEM((heads, ch), F32),
        ),
        in_specs=[pl.BlockSpec(memory_space=pltpu.HBM)] * 7,
        out_specs=(vm,) * 6,
        scratch_shapes=[
            *(pltpu.VMEM(v.shape, v.dtype) for v in operands),
            dma((7,)),
            pltpu.VMEM((cg, groups * tc), F32),
            pltpu.VMEM((tr + 32, ch), F32),
            pltpu.VMEM((tc + 32, ch), F32),
            pltpu.VMEM((tr + 16, ch), F32),
            pltpu.VMEM((tc + 16, ch), F32),
            pltpu.VMEM((2 * ch, lanes), F32),
            pltpu.VMEM((tr, 8 * ch), BF),
            pltpu.VMEM((8 * ch, tc), BF),
            pltpu.VMEM((cg + ch, hg), BF),
            pltpu.VMEM((cg, 8 * ch), BF),
            pltpu.VMEM((2, 2 * tc, 8 * ch), BF),
            pltpu.VMEM((2, ch, cg), BF),
            pltpu.VMEM((ch, 8, 2 * tc), F32),
            pltpu.VMEM((2, cg, 2 * tc), F32),
            pltpu.VMEM((n_row, tr, d), BF),
            dma((n_row,)), dma((n_row,)),
            pltpu.VMEM((tr, 4 * ch), F32),
            pltpu.VMEM((ch, tc), F32),
            pltpu.VMEM((cg, groups * tc), BF),
            pltpu.VMEM((cg, groups * tc), BF),
            pltpu.VMEM((hg, groups * tc), BF),
            pltpu.VMEM((tr + 32, 4 * ch), F32),
            pltpu.VMEM((tc + 32, 4 * ch), F32),
            pltpu.VMEM((tr, lanes), BF),
            pltpu.VMEM((2, 16, lanes), BF),
            pltpu.VMEM((tc + 32, lanes), BF),
            pltpu.VMEM((n_col, pp, lanes), F32),
            pltpu.VMEM((n_col, pp, lanes), F32),
            pltpu.VMEM((pr, lanes), F32),
            pltpu.VMEM((n_row, pr, lanes), F32),
            pltpu.VMEM((2, 8, lanes), F32),
            pltpu.VMEM((2, 8, lanes), F32),
            pltpu.VMEM((n_col, sp, lanes), F32),
            pltpu.VMEM((n_col, sp, lanes), F32),
            dma((n_col,)), dma((n_col,)),
            pltpu.VMEM((ag, lanes), BF),
            pltpu.VMEM((n_col, ag, lanes), BF),
            pltpu.VMEM((sp, lanes), F32),
            pltpu.VMEM((n_row, sp, lanes), F32),
            pltpu.VMEM((n_col, sp, lanes), F32),
            pltpu.VMEM((2 * ch, tr), BF),
            pltpu.VMEM((n_row, 2 * ch, tr), BF),
            pltpu.VMEM((tr + 2 * tc + 16, ch), F32),
            dma((3, n_row)), dma((3,)), dma((2,)), dma((2,)),
            dma((n_col,)), dma((n_col,)), dma((n_row,)), dma((n_row,)), dma((2,)), dma((2,)),
            dma((n_col,)), dma((n_col,)), dma((n_row,)), dma((n_row,)),
            dma((n_col,)), dma((n_col,)), dma((n_row,)), dma((n_row,)),
            dma((3,)),
        ],
        compiler_params=pltpu.CompilerParams(
            vmem_limit_bytes=63 * 1024 * 1024, collective_id=0, has_side_effects=True),
    )(*operands)
    hbm = pl.BlockSpec(memory_space=pltpu.HBM)
    gf, gwl, gwr, gk, gp, gh = pl.pallas_call(
        move_kernel,
        out_shape=tuple(jax.ShapeDtypeStruct(v.shape, v.dtype) for v in outs),
        in_specs=[vm] * 6,
        out_specs=(hbm,) * 6,
        scratch_shapes=[dma((6,))],
        compiler_params=pltpu.CompilerParams(vmem_limit_bytes=16 * 1024 * 1024),
    )(*outs)
    return gf, gwl.T, gwr.T, gk, gp, gh.T


def solution(mesh):
    return jax.shard_map(
        body,
        mesh=mesh,
        in_specs=(P("row", None), P(), P(), P(), P(), P(), P(None, "row", "col")),
        out_specs=(P("row", None), P(), P(), P(), P(), P()),
        check_vma=False,
    )
```

```python
import functools
import math

import jax
import jax.numpy as jnp
from jax import lax
from jax.experimental import pallas as pl
from jax.experimental.pallas import tpu as pltpu
from jax.sharding import PartitionSpec as P

STEP = 4
BF = jnp.bfloat16
F32 = jnp.float32
HI = lax.Precision.HIGHEST
GR = 16


def iota(shape, dim):
    return lax.broadcasted_iota(jnp.int32, shape, dim)


def split(x):
    hi = x.astype(BF)
    return hi, (x - hi.astype(F32)).astype(BF)


def dotf(a, b, contract=((1,), (0,)), precision=None):
    return lax.dot_general(a, b, (contract, ((), ())), precision=precision, preferred_element_type=F32)


MESH = pl.DeviceIdType.MESH


def pack(x):
    n = x.shape[0] // 4
    return jnp.concatenate([x[k * n : (k + 1) * n] for k in range(4)], axis=1)


def unpack(x):
    n = x.shape[1] // 4
    return jnp.concatenate([x[:, k * n : (k + 1) * n] for k in range(4)], axis=0)


def tile_kernel(scale, feats_hbm, wl_hbm, wr_hbm, dk_hbm, wp_hbm, wh_hbm, cot_hbm,
                gf_out, gwl_out, gwr_out, gk_out, gp_out, gh_out,
                feats, wl, wr, dk, wp, wh, cot, load_sem, ghs,
                lext, rext, plx, prx, small, qs, ns, k2, cm, es, ecol, colsum, us, rs, cs, gcs, hid, xs, zl, zr,
                proj, lbuf, rbuf, colsend, colrecv, rowsend, rowrecv, halosend, halorecv,
                smsend, smrecv, m1s, m1r,
                agsend, agrecv, spsend, sprecv, sfin, gwsend, gwrecv, window,
                rseg_send, rseg_recv, lseg_send, lseg_recv, c1s, c1r, r1s, r1r, h1s, h1r,
                c2s, c2r, r2s, r2r, c3s, c3r, r3s, r3r, local_sem):
    loads = [pltpu.make_async_copy(src, dst, load_sem.at[k]) for k, (src, dst) in enumerate((
        (feats_hbm, feats), (wl_hbm, wl), (wr_hbm, wr), (dk_hbm, dk), (wp_hbm, wp), (wh_hbm, wh), (cot_hbm, cot)))]
    for copy in loads:
        copy.start()
    heads, ch = wh.shape
    tr, tc = cot.shape[1:]
    groups = tr // GR
    cg, hg = ch * GR, heads * GR
    row, col = lax.axis_index("row"), lax.axis_index("col")
    row_first, row_last = row == 0, row == lax.axis_size("row") - 1
    col_first, col_last = col == 0, col == lax.axis_size("col") - 1
    def edge(first, last, pos, length):
        return ((pos < STEP) & first) | ((pos >= length - STEP) & last)

    n_row, n_col = lax.axis_size("row"), lax.axis_size("col")
    nb = tr * n_row
    row_mates = [lax.rem(row + k, n_row) for k in range(1, n_row)]
    col_mates = [lax.rem(col + k, n_col) for k in range(1, n_col)]

    lbuf[...] = jnp.zeros_like(lbuf)
    halorecv[...] = jnp.zeros_like(halorecv)
    for first, count in ((0, 16), (16 + tc, 16)):
        rbuf[first : first + count, :] = jnp.zeros((count, 4 * ch), BF)
    barrier = pltpu.get_barrier_semaphore()
    for m in row_mates:
        pl.semaphore_signal(barrier, inc=1, device_id=(m, col), device_id_type=MESH)
    for m in col_mates:
        pl.semaphore_signal(barrier, inc=1, device_id=(row, m), device_id_type=MESH)

    for copy in loads[:6]:
        copy.wait()
    taps = [[dk[3 * a + b : 3 * a + b + 1, :] for b in range(3)] for a in range(3)]

    weights = jnp.concatenate([wl[...], wr[...], jnp.zeros((2 * ch, wl.shape[1]), BF)], axis=0)
    proj[...] = dotf(feats[...], weights, ((1,), (1,))).astype(BF)
    pl.semaphore_wait(barrier, n_row + n_col - 2)

    def remote(src, dst, send, recv, device):
        return pltpu.make_async_remote_copy(
            src_ref=src, dst_ref=dst, send_sem=send, recv_sem=recv, device_id=device, device_id_type=MESH)

    up = remote(proj.at[pl.ds(0, 16)], lbuf.at[1], lseg_send.at[0], lseg_recv.at[1], (row - 1, col))
    down = remote(proj.at[pl.ds(tr - 16, 16)], lbuf.at[0], lseg_send.at[1], lseg_recv.at[0], (row + 1, col))
    pl.when(row > 0)(up.start)
    pl.when(row < n_row - 1)(down.start)
    segments = []
    for k, (offset, first, count) in enumerate(((-16, 0, 16), (0, 16, tc), (tc, 16 + tc, 16))):
        bin0 = col * tc + offset
        inside = (bin0 >= 0) & (bin0 < nb)
        owner = lax.div(bin0 + nb, tr) - n_row
        local = pl.multiple_of(lax.rem(bin0 + nb, tr), 16)
        src = proj.at[pl.ds(local, count)]
        dst = rbuf.at[pl.ds(first, count)]
        own = inside & (owner == row)
        copies = [remote(src, dst, rseg_send.at[k, i], rseg_recv.at[k], (m, col)) for i, m in enumerate(row_mates)]
        keep = pltpu.make_async_copy(src, dst, local_sem.at[k])
        segments.append((inside, own, copies, keep))

        @pl.when(own)
        def _(copies=copies, keep=keep):
            for c in copies:
                c.start()
            keep.start()

    cm[...] = jnp.where(iota((cg, 8 * ch), 0) // GR == iota((cg, 8 * ch), 1) % ch, 1.0, 0.0).astype(BF)

    w2 = (0.5 * scale * dotf(wp[...], wh[...], ((1,), (1,)))).astype(BF)
    e_r = jnp.where(iota((cg, ch), 0) // GR == iota((cg, ch), 1), 1.0, 0.0).astype(BF)
    e_c = jnp.where(iota((heads, hg), 1) // GR == iota((heads, hg), 0), 1.0, 0.0).astype(BF)
    w2r = dotf(e_r, w2).astype(BF)
    same = iota((cg, hg), 0) % GR == iota((cg, hg), 1) % GR
    k2[:cg, :] = jnp.where(same, dotf(w2r, e_c), 0.0).astype(BF)
    k2[cg:, :] = jnp.where(iota((ch, hg), 0) == iota((ch, hg), 1) // GR, 1.0, 0.0).astype(BF)

    jj, part = iota((2 * tc, 8 * ch), 0), iota((2 * tc, 8 * ch), 1)
    paired = jj // tc == part // (4 * ch)
    jj, part = jj % tc, part % (4 * ch) // ch
    drop = ((part == 0) & (jj < STEP) & col_first) | ((part == 2) & (jj >= tc - STEP) & col_last)
    es[0] = jnp.where(paired & ~drop & (part != 3), 1.0, 0.0).astype(BF)
    es[1] = jnp.where(paired & (part == 3), 1.0, 0.0).astype(BF)
    pr, ci = iota((ch, cg), 0), iota((ch, cg), 1)
    mine = pr == ci // GR
    ecol[0] = jnp.where(mine & (ci % GR < STEP) & row_first, 1.0, 0.0).astype(BF)
    ecol[1] = jnp.where(mine & (ci % GR >= GR - STEP) & row_last, 1.0, 0.0).astype(BF)
    colsum[...] = jnp.zeros_like(colsum)
    cs[...] = jnp.zeros_like(cs)
    lane_c = iota((1, 1, 8 * ch), 2) % ch
    loads[6].wait()

    def ahead(g, carry):
        start = pl.multiple_of(g * 2 * GR, 2 * GR)
        lanes = pl.ds(pl.multiple_of(g * 2 * tc, 256), 2 * tc)
        x = jnp.concatenate(
            [cot[:, pl.ds(start + k * GR, GR), :].reshape(hg, tc) for k in range(2)], axis=1)
        xs[:, lanes] = x
        w = dotf(k2[...], x)
        ghs[:, lanes] = w[:cg]
        cs[...] += w[cg:, :tc] + w[cg:, tc:]
        y = dotf(x, es[1]).reshape(heads, GR, 8 * ch)
        y = jnp.sum(jnp.where(iota((heads, 1, 8 * ch), 0) == lane_c, y, 0.0), axis=0)
        rs[pl.ds(start, GR), :] = y[:, : 4 * ch]
        rs[pl.ds(start + GR, GR), :] = y[:, 4 * ch :]
        return carry

    lax.fori_loop(0, groups // 2, ahead, 0)

    for inside, own, copies, keep in segments:

        @pl.when(own)
        def _(copies=copies, keep=keep):
            keep.wait()
            for c in copies:
                c.wait_send()

        @pl.when(inside & jnp.logical_not(own))
        def _(copies=copies):
            copies[0].wait_recv()

    @pl.when(row > 0)
    def _():
        up.wait_send()
        down.wait_recv()

    @pl.when(row < n_row - 1)
    def _():
        down.wait_send()
        up.wait_recv()

    lext[0:16, :] = lbuf[0, :, :ch].astype(F32)
    lext[16 : 16 + tr, :] = proj[:, :ch].astype(F32)
    lext[16 + tr :, :] = lbuf[1, :, :ch].astype(F32)
    rext[...] = rbuf[:, ch : 2 * ch].astype(F32)

    l_sh = [lext[16 + STEP * (a - 1) : 16 + STEP * (a - 1) + tr, :] for a in range(3)]
    r_sh = [rext[16 + STEP * (b - 1) : 16 + STEP * (b - 1) + tc, :] for b in range(3)]
    a1 = sum(l_sh[a] * (taps[a][0] + taps[a][1] + taps[a][2]) for a in range(3))
    da0 = sum(l_sh[a] * taps[a][0] for a in range(3))
    da2 = sum(l_sh[a] * taps[a][2] for a in range(3))
    da = -jnp.where(col_first, da0, jnp.where(col_last, da2, jnp.zeros_like(da2)))
    b1 = sum(r_sh[b] * (taps[0][b] + taps[1][b] + taps[2][b]) for b in range(3))
    db0 = sum(r_sh[b] * taps[0][b] for b in range(3))
    db2 = sum(r_sh[b] * taps[2][b] for b in range(3))
    db = -jnp.where(row_first, db0, jnp.where(row_last, db2, jnp.zeros_like(db2)))
    rind = jnp.where(edge(row_first, row_last, iota((tr, 2 * ch), 0), tr), 1.0, 0.0).astype(BF)
    qs[...] = jnp.concatenate(
        [*split(0.5 * a1), *split(0.5 * da), jnp.ones((tr, 2 * ch), BF), rind], axis=1)
    b_parts = [p.astype(F32) for p in (*split(0.5 * b1), *split(0.5 * db))]
    ns[4 * ch :, :] = jnp.concatenate(b_parts, axis=1).T.astype(BF)
    ns[: 2 * ch, :] = jnp.ones((2 * ch, tc), BF)
    ns[2 * ch : 4 * ch, :] = jnp.where(
        edge(col_first, col_last, iota((2 * ch, tc), 1), tc), 1.0, 0.0).astype(BF)

    chunk = 64
    n = chunk // GR

    def pair(g, slot):
        start = pl.multiple_of(g * 2 * GR, 2 * GR)
        mask = cm[...].reshape(ch, GR, 8 * ch)
        for j in range(2):
            q = qs[pl.ds(start + j * GR, GR), :]
            us[slot, :, j * tc : (j + 1) * tc] = dotf((mask * q[None]).reshape(cg, 8 * ch), ns[...])
        lanes = pl.ds(pl.multiple_of(g * 2 * tc, 256), 2 * tc)
        for k in range(cg // chunk):
            rows = slice(k * chunk, (k + 1) * chunk)
            u = us[slot, rows, :]
            t = jnp.tanh(u)
            p = 1.0 + t
            h = u * p
            hid[rows, lanes] = h.astype(BF)
            gc = ghs[rows, lanes] * (p + h - h * t)
            gcs[rows, lanes] = gc.astype(BF)
            colsum[k * n : (k + 1) * n] += jnp.sum(gc.reshape(n, 2, 8, 2 * tc), axis=1)
        y = dotf(gcs[:, lanes], es[0]).reshape(ch, GR, 8 * ch)
        total = jnp.sum(jnp.where(iota((ch, 1, 8 * ch), 0) == lane_c, y, 0.0), axis=0)
        rs[pl.ds(start, GR), :] += total[:, : 4 * ch]
        rs[pl.ds(start + GR, GR), :] += total[:, 4 * ch :]

    def group(g, carry):
        pair(2 * g, 0)
        pair(2 * g + 1, 1)
        return carry

    lax.fori_loop(0, groups // 4, group, 0)
    base = jnp.sum(colsum[...], axis=1)
    base = base[:, :tc] + base[:, tc:]
    top = dotf(ecol[0], gcs[:, :tc])
    low = dotf(ecol[1], gcs[:, (groups - 1) * tc :])
    cst = jnp.concatenate([base - top, base, base - low, cs[...]], axis=0).T
    rsv = rs[...]
    eye = iota((ch, ch), 0) == iota((ch, ch), 1)
    whs = scale * jnp.concatenate([wh[...].astype(F32), jnp.zeros((ch - heads, ch), F32)], axis=0)
    zc = jnp.zeros((ch, ch), F32)

    def spread(tap):
        blocks = [[jnp.where(eye, tap(n, m), 0.0) for m in range(3)] + [zc] for n in range(3)]
        blocks.append([zc, zc, zc, whs])
        return jnp.concatenate([jnp.concatenate(b, axis=1) for b in blocks], axis=0)

    for sums, z, out, length, weights in (
        (rsv, zl, plx, tr, spread(lambda b, a: taps[a][b])),
        (cst, zr, prx, tc, spread(lambda a, b: taps[a][b])),
    ):
        z[:16, :] = jnp.zeros((16, 4 * ch), F32)
        z[16 + length :, :] = jnp.zeros((16, 4 * ch), F32)
        z[16 : 16 + length, :] = dotf(sums, weights, precision=HI)
        ext = z[8 : 24 + length, 3 * ch :]
        for n in range(3):
            ext = ext + z[12 - STEP * n : 28 - STEP * n + length, n * ch : (n + 1) * ch]
        out[...] = ext

    lanes = 4 * ch
    pp, sp = tr // 4 // n_col, 2 * ch // n_col
    colsend[...] = pack(plx[8 : 8 + tr, :]).reshape(n_col, pp, lanes)
    pad = jnp.zeros((8, 3 * ch), F32)
    halosend[0] = jnp.concatenate([plx[:8, :], pad], axis=1)
    halosend[1] = jnp.concatenate([plx[8 + tr :, :], pad], axis=1)
    pr = (tc + 16) // 4
    rowsend[...] = pack(prx[...])

    def to_col(src, dst, send, recv):
        return [remote(src(m), dst.at[col], send.at[m], recv.at[col], (row, m)) for m in col_mates]

    def to_row(src, dst, send, recv):
        return [remote(src, dst.at[row], send.at[m], recv.at[row], (m, col)) for m in row_mates]

    def from_col(src, dst, send, recv):
        return [remote(src(m), dst.at[m], send.at[m], recv.at[m], (row, m)) for m in col_mates]

    def from_row(src, dst, send, recv):
        return [remote(src, dst.at[m], send.at[m], recv.at[m], (m, col)) for m in row_mates]

    def start(copies):
        for c in copies:
            c.start()

    def arrived(copies):
        for c in copies:
            c.wait_recv()

    def sent(copies):
        for c in copies:
            c.wait_send()

    hup = remote(halosend.at[0], halorecv.at[1], h1s.at[0], h1r.at[1], (row - 1, col))
    hdown = remote(halosend.at[1], halorecv.at[0], h1s.at[1], h1r.at[0], (row + 1, col))
    p1c = (lambda m: colsend.at[m], colrecv, c1s, c1r)
    p1r = (rowsend, rowrecv, r1s, r1r)
    s1c, s1r = to_col(*p1c), to_row(*p1r)
    start(s1c)
    start(s1r)
    pl.when(row > 0)(hup.start)
    pl.when(row < n_row - 1)(hdown.start)
    prod = dotf(hid[...], xs[...], ((1,), (1,)))
    prod = jnp.sum(jnp.where(same, prod, 0.0).reshape(ch, GR, hg), axis=1)
    e_h = jnp.where(iota((hg, ch), 0) // GR == iota((hg, ch), 1), 1.0, 0.0)
    hc = dotf(prod, e_h, precision=HI)
    pc = dotf(l_sh[1], rsv[:, 3 * ch :], ((0,), (0,)), HI) + dotf(r_sh[1], cst[:, 3 * ch :], ((0,), (0,)), HI)
    small[:ch, :] = jnp.concatenate([hc, pc, jnp.zeros((ch, 2 * ch), F32)], axis=1)
    rows_out = []
    zero_l, zero_r = jnp.zeros((tr, ch), F32), jnp.zeros((tc, ch), F32)
    for a in range(3):
        rows_out.append(jnp.sum(jnp.concatenate([l_sh[a]] * 3 + [zero_l], axis=1) * rsv, axis=0, keepdims=True))
    for b in range(3):
        rows_out.append(jnp.sum(jnp.concatenate([r_sh[b]] * 3 + [zero_r], axis=1) * cst, axis=0, keepdims=True))
    small[ch : ch + 8, :] = jnp.concatenate(rows_out + [jnp.zeros((2, 4 * ch), F32)], axis=0)
    small[ch + 8 :, :] = jnp.zeros((ch - 8, 4 * ch), F32)
    smsend[...] = small[...].reshape(n_col, sp, lanes)
    p1s = (lambda m: smsend.at[m], smrecv, m1s, m1r)
    s1s = to_col(*p1s)
    start(s1s)
    arrived(from_col(*p1c))
    piece = colsend[col]
    for m in col_mates:
        piece = piece + colrecv[m]
    arrived(from_row(*p1r))
    right = rowsend[...]
    for m in row_mates:
        right = right + rowrecv[m]

    @pl.when(row > 0)
    def _():
        hup.wait_send()
        hdown.wait_recv()

    @pl.when(row < n_row - 1)
    def _():
        hdown.wait_send()
        hup.wait_recv()

    fill = [jnp.zeros((agsend.shape[0] - pp - 4 - pr, lanes), F32)] if agsend.shape[0] > pp + 4 + pr else []
    agsend[...] = jnp.concatenate(
        [right, pack(halorecv[0, :, :ch]), pack(halorecv[1, :, :ch]), piece] + fill, axis=0).astype(BF)
    p2c = (lambda m: agsend, agrecv, c2s, c2r)
    s2c = to_col(*p2c)
    start(s2c)
    arrived(from_col(*p1s))
    part = smsend[col]
    for m in col_mates:
        part = part + smrecv[m]
    spsend[...] = part
    p2r = (spsend, sprecv, r2s, r2r)
    s2r = to_row(*p2r)
    start(s2r)
    sent(s1c)
    sent(s1r)
    sent(s1s)
    arrived(from_col(*p2c))
    sent(s2c)
    agrecv[col] = agsend[...]
    gl = unpack(jnp.concatenate([agrecv[m, pr + 4 : pr + 4 + pp, :].astype(F32) for m in range(n_col)], axis=0))
    halo = sum(agrecv[m, pr : pr + 4, :].astype(F32) for m in range(n_col))
    gl = jnp.concatenate([gl[:8] + unpack(halo[:2]), gl[8:-8], gl[-8:] + unpack(halo[2:])], axis=0)
    window[...] = jnp.zeros_like(window)
    for k in range(tr // tc + 2):
        m = lax.div(row * tr, tc) - 1 + k

        @pl.when((m >= 0) & (m < n_col))
        def _(m=m, k=k):
            window[k * tc : k * tc + tc + 16, :] += unpack(agrecv[m, :pr, :].astype(F32))

    gr = window[tc + 8 : tc + 8 + tr, :]
    glb, grb = gl.astype(BF), gr.astype(BF)
    both = jnp.concatenate([gl, gr, jnp.zeros((tr, 2 * ch), F32)], axis=1).T[: 2 * ch].astype(BF)

    part = scale * dotf(both, feats[...])
    gwsend[...] = part.astype(BF)
    p3r = (gwsend, gwrecv, r3s, r3r)
    s3r = to_row(*p3r)
    start(s3r)
    arrived(from_row(*p2r))
    total = spsend[...]
    for m in row_mates:
        total = total + sprecv[m]
    sfin[col] = total
    p3c = (lambda m: sfin.at[col], sfin, c3s, c3r)
    s3c = to_col(*p3c)
    start(s3c)
    gf_out[...] = (dotf(glb, wl[...]) + dotf(grb, wr[...])).astype(BF)
    arrived(from_col(*p3c))
    sent(s3c)
    sent(s2r)
    full = jnp.concatenate([sfin[m] for m in range(n_col)], axis=0)
    hc, pc = full[:ch, :heads], full[:ch, ch : ch + heads]
    for a in range(3):
        for b in range(3):
            gk_out[3 * a + b : 3 * a + b + 1, :] = scale * (
                full[ch + a : ch + a + 1, b * ch : (b + 1) * ch]
                + full[ch + 3 + b : ch + 4 + b, a * ch : (a + 1) * ch])
    gp_out[...] = scale * scale * dotf(hc, wh[...].astype(F32), precision=HI)
    gh_out[...] = (scale * (pc + dotf(wp[...].astype(F32), hc, ((0,), (0,)), HI))).T
    arrived(from_row(*p3r))
    for m in row_mates:
        part = part + gwrecv[m].astype(F32)
    gwl_out[...] = part[:ch]
    gwr_out[...] = part[ch:]
    sent(s3r)


def move_kernel(*refs):
    sems = refs[-1]
    n = len(refs) // 2
    copies = [pltpu.make_async_copy(refs[k], refs[n + k], sems.at[k]) for k in range(n)]
    for c in copies:
        c.start()
    for c in copies:
        c.wait()


def body(bin_features, w_left, w_right, depth_kernel, w_point, w_head, cotangent):
    ch, heads = w_head.shape
    tr, tc = cotangent.shape[1:]
    n_row, n_col = lax.axis_size("row"), lax.axis_size("col")
    scale = 1.0 / math.sqrt(tr * n_row)
    cg, hg, groups = ch * GR, heads * GR, tr // GR
    d, lanes = w_left.shape[0], 4 * ch
    pp, sp, pr = tr // 4 // n_col, 2 * ch // n_col, (tc + 16) // 4
    ag = -(-(pp + 4 + pr) // 16) * 16
    vm = pl.BlockSpec(memory_space=pltpu.VMEM)
    dma = pltpu.SemaphoreType.DMA
    operands = (bin_features, w_left.T, w_right.T, depth_kernel, w_point, w_head.T, cotangent)
    outs = pl.pallas_call(
        functools.partial(tile_kernel, scale),
        out_shape=(
            pltpu.VMEM((tr, d), BF),
            pltpu.VMEM((ch, d), F32),
            pltpu.VMEM((ch, d), F32),
            pltpu.VMEM((9, ch), F32),
            pltpu.VMEM((ch, ch), F32),
            pltpu.VMEM((heads, ch), F32),
        ),
        in_specs=[pl.BlockSpec(memory_space=pltpu.HBM)] * 7,
        out_specs=(vm,) * 6,
        scratch_shapes=[
            *(pltpu.VMEM(v.shape, v.dtype) for v in operands),
            dma((7,)),
            pltpu.VMEM((cg, groups * tc), F32),
            pltpu.VMEM((tr + 32, ch), F32),
            pltpu.VMEM((tc + 32, ch), F32),
            pltpu.VMEM((tr + 16, ch), F32),
            pltpu.VMEM((tc + 16, ch), F32),
            pltpu.VMEM((2 * ch, lanes), F32),
            pltpu.VMEM((tr, 8 * ch), BF),
            pltpu.VMEM((8 * ch, tc), BF),
            pltpu.VMEM((cg + ch, hg), BF),
            pltpu.VMEM((cg, 8 * ch), BF),
            pltpu.VMEM((2, 2 * tc, 8 * ch), BF),
            pltpu.VMEM((2, ch, cg), BF),
            pltpu.VMEM((ch, 8, 2 * tc), F32),
            pltpu.VMEM((2, cg, 2 * tc), F32),
            pltpu.VMEM((tr, 4 * ch), F32),
            pltpu.VMEM((ch, tc), F32),
            pltpu.VMEM((cg, groups * tc), BF),
            pltpu.VMEM((cg, groups * tc), BF),
            pltpu.VMEM((hg, groups * tc), BF),
            pltpu.VMEM((tr + 32, 4 * ch), F32),
            pltpu.VMEM((tc + 32, 4 * ch), F32),
            pltpu.VMEM((tr, lanes), BF),
            pltpu.VMEM((2, 16, lanes), BF),
            pltpu.VMEM((tc + 32, lanes), BF),
            pltpu.VMEM((n_col, pp, lanes), F32),
            pltpu.VMEM((n_col, pp, lanes), F32),
            pltpu.VMEM((pr, lanes), F32),
            pltpu.VMEM((n_row, pr, lanes), F32),
            pltpu.VMEM((2, 8, lanes), F32),
            pltpu.VMEM((2, 8, lanes), F32),
            pltpu.VMEM((n_col, sp, lanes), F32),
            pltpu.VMEM((n_col, sp, lanes), F32),
            dma((n_col,)), dma((n_col,)),
            pltpu.VMEM((ag, lanes), BF),
            pltpu.VMEM((n_col, ag, lanes), BF),
            pltpu.VMEM((sp, lanes), F32),
            pltpu.VMEM((n_row, sp, lanes), F32),
            pltpu.VMEM((n_col, sp, lanes), F32),
            pltpu.VMEM((2 * ch, d), BF),
            pltpu.VMEM((n_row, 2 * ch, d), BF),
            pltpu.VMEM((tr + 2 * tc + 16, ch), F32),
            dma((3, n_row)), dma((3,)), dma((2,)), dma((2,)),
            dma((n_col,)), dma((n_col,)), dma((n_row,)), dma((n_row,)), dma((2,)), dma((2,)),
            dma((n_col,)), dma((n_col,)), dma((n_row,)), dma((n_row,)),
            dma((n_col,)), dma((n_col,)), dma((n_row,)), dma((n_row,)),
            dma((3,)),
        ],
        compiler_params=pltpu.CompilerParams(
            vmem_limit_bytes=63 * 1024 * 1024, collective_id=0, has_side_effects=True),
    )(*operands)
    hbm = pl.BlockSpec(memory_space=pltpu.HBM)
    gf, gwl, gwr, gk, gp, gh = pl.pallas_call(
        move_kernel,
        out_shape=tuple(jax.ShapeDtypeStruct(v.shape, v.dtype) for v in outs),
        in_specs=[vm] * 6,
        out_specs=(hbm,) * 6,
        scratch_shapes=[dma((6,))],
        compiler_params=pltpu.CompilerParams(vmem_limit_bytes=16 * 1024 * 1024),
    )(*outs)
    return gf, gwl.T, gwr.T, gk, gp, gh.T


def solution(mesh):
    return jax.shard_map(
        body,
        mesh=mesh,
        in_specs=(P("row", None), P(), P(), P(), P(), P(), P(None, "row", "col")),
        out_specs=(P("row", None), P(), P(), P(), P(), P()),
        check_vma=False,
    )
```

```python
import functools
import math

import jax
import jax.numpy as jnp
from jax import lax
from jax.experimental import pallas as pl
from jax.experimental.pallas import tpu as pltpu
from jax.sharding import PartitionSpec as P

STEP = 4
BF = jnp.bfloat16
F32 = jnp.float32
HI = lax.Precision.HIGHEST
GR = 16


def iota(shape, dim):
    return lax.broadcasted_iota(jnp.int32, shape, dim)


def split(x):
    hi = x.astype(BF)
    return hi, (x - hi.astype(F32)).astype(BF)


def dotf(a, b, contract=((1,), (0,)), precision=None):
    return lax.dot_general(a, b, (contract, ((), ())), precision=precision, preferred_element_type=F32)


MESH = pl.DeviceIdType.MESH


def pack(x):
    n = x.shape[0] // 4
    return jnp.concatenate([x[k * n : (k + 1) * n] for k in range(4)], axis=1)


def unpack(x):
    n = x.shape[1] // 4
    return jnp.concatenate([x[:, k * n : (k + 1) * n] for k in range(4)], axis=0)


def tile_kernel(scale, feats_hbm, wl_hbm, wr_hbm, dk_hbm, wp_hbm, wh_hbm, cot_hbm,
                gf_out, gwl_out, gwr_out, gk_out, gp_out, gh_out,
                feats, wl, wr, dk, wp, wh, cot, load_sem, ghs,
                lext, rext, plx, prx, small, qs, ns, k2, cm, es, ecol, colsum, us, rs, cs, gcs, hid, xs, zl, zr,
                proj, lbuf, rbuf, colsend, colrecv, rowsend, rowrecv, halosend, halorecv,
                smsend, smrecv, m1s, m1r,
                agsend, agrecv, spsend, sprecv, sfin, gwsend, gwrecv, window,
                rseg_send, rseg_recv, lseg_send, lseg_recv, c1s, c1r, r1s, r1r, h1s, h1r,
                c2s, c2r, r2s, r2r, c3s, c3r, r3s, r3r, local_sem):
    loads = [pltpu.make_async_copy(src, dst, load_sem.at[k]) for k, (src, dst) in enumerate((
        (feats_hbm, feats), (wl_hbm, wl), (wr_hbm, wr), (dk_hbm, dk), (wp_hbm, wp), (wh_hbm, wh), (cot_hbm, cot)))]
    for copy in loads:
        copy.start()
    heads, ch = wh.shape
    tr, tc = cot.shape[1:]
    groups = tr // GR
    cg, hg = ch * GR, heads * GR
    row, col = lax.axis_index("row"), lax.axis_index("col")
    row_first, row_last = row == 0, row == lax.axis_size("row") - 1
    col_first, col_last = col == 0, col == lax.axis_size("col") - 1
    def edge(first, last, pos, length):
        return ((pos < STEP) & first) | ((pos >= length - STEP) & last)

    n_row, n_col = lax.axis_size("row"), lax.axis_size("col")
    nb = tr * n_row
    row_mates = [lax.rem(row + k, n_row) for k in range(1, n_row)]
    col_mates = [lax.rem(col + k, n_col) for k in range(1, n_col)]

    lbuf[...] = jnp.zeros_like(lbuf)
    halorecv[...] = jnp.zeros_like(halorecv)
    for first, count in ((0, 16), (16 + tc, 16)):
        rbuf[first : first + count, :] = jnp.zeros((count, 4 * ch), BF)
    barrier = pltpu.get_barrier_semaphore()
    for m in row_mates:
        pl.semaphore_signal(barrier, inc=1, device_id=(m, col), device_id_type=MESH)
    for m in col_mates:
        pl.semaphore_signal(barrier, inc=1, device_id=(row, m), device_id_type=MESH)

    for copy in loads[:6]:
        copy.wait()
    taps = [[dk[3 * a + b : 3 * a + b + 1, :] for b in range(3)] for a in range(3)]

    weights = jnp.concatenate([wl[...], wr[...], jnp.zeros((2 * ch, wl.shape[1]), BF)], axis=0)
    proj[...] = dotf(feats[...], weights, ((1,), (1,))).astype(BF)
    pl.semaphore_wait(barrier, n_row + n_col - 2)

    def remote(src, dst, send, recv, device):
        return pltpu.make_async_remote_copy(
            src_ref=src, dst_ref=dst, send_sem=send, recv_sem=recv, device_id=device, device_id_type=MESH)

    up = remote(proj.at[pl.ds(0, 16)], lbuf.at[1], lseg_send.at[0], lseg_recv.at[1], (row - 1, col))
    down = remote(proj.at[pl.ds(tr - 16, 16)], lbuf.at[0], lseg_send.at[1], lseg_recv.at[0], (row + 1, col))
    pl.when(row > 0)(up.start)
    pl.when(row < n_row - 1)(down.start)
    segments = []
    for k, (offset, first, count) in enumerate(((-16, 0, 16), (0, 16, tc), (tc, 16 + tc, 16))):
        bin0 = col * tc + offset
        inside = (bin0 >= 0) & (bin0 < nb)
        owner = lax.div(bin0 + nb, tr) - n_row
        local = pl.multiple_of(lax.rem(bin0 + nb, tr), 16)
        src = proj.at[pl.ds(local, count)]
        dst = rbuf.at[pl.ds(first, count)]
        own = inside & (owner == row)
        copies = [remote(src, dst, rseg_send.at[k, i], rseg_recv.at[k], (m, col)) for i, m in enumerate(row_mates)]
        keep = pltpu.make_async_copy(src, dst, local_sem.at[k])
        segments.append((inside, own, copies, keep))

        @pl.when(own)
        def _(copies=copies, keep=keep):
            for c in copies:
                c.start()
            keep.start()

    cm[...] = jnp.where(iota((cg, 8 * ch), 0) // GR == iota((cg, 8 * ch), 1) % ch, 1.0, 0.0).astype(BF)

    w2 = (0.5 * scale * dotf(wp[...], wh[...], ((1,), (1,)))).astype(BF)
    e_r = jnp.where(iota((cg, ch), 0) // GR == iota((cg, ch), 1), 1.0, 0.0).astype(BF)
    e_c = jnp.where(iota((heads, hg), 1) // GR == iota((heads, hg), 0), 1.0, 0.0).astype(BF)
    w2r = dotf(e_r, w2).astype(BF)
    same = iota((cg, hg), 0) % GR == iota((cg, hg), 1) % GR
    k2[:cg, :] = jnp.where(same, dotf(w2r, e_c), 0.0).astype(BF)
    k2[cg:, :] = jnp.where(iota((ch, hg), 0) == iota((ch, hg), 1) // GR, 1.0, 0.0).astype(BF)

    jj, part = iota((2 * tc, 8 * ch), 0), iota((2 * tc, 8 * ch), 1)
    paired = jj // tc == part // (4 * ch)
    jj, part = jj % tc, part % (4 * ch) // ch
    drop = ((part == 0) & (jj < STEP) & col_first) | ((part == 2) & (jj >= tc - STEP) & col_last)
    es[0] = jnp.where(paired & ~drop & (part != 3), 1.0, 0.0).astype(BF)
    es[1] = jnp.where(paired & (part == 3), 1.0, 0.0).astype(BF)
    pr, ci = iota((ch, cg), 0), iota((ch, cg), 1)
    mine = pr == ci // GR
    ecol[0] = jnp.where(mine & (ci % GR < STEP) & row_first, 1.0, 0.0).astype(BF)
    ecol[1] = jnp.where(mine & (ci % GR >= GR - STEP) & row_last, 1.0, 0.0).astype(BF)
    colsum[...] = jnp.zeros_like(colsum)
    cs[...] = jnp.zeros_like(cs)
    lane_c = iota((1, 1, 8 * ch), 2) % ch
    loads[6].wait()

    def ahead(g, carry):
        start = pl.multiple_of(g * 2 * GR, 2 * GR)
        lanes = pl.ds(pl.multiple_of(g * 2 * tc, 256), 2 * tc)
        x = jnp.concatenate(
            [cot[:, pl.ds(start + k * GR, GR), :].reshape(hg, tc) for k in range(2)], axis=1)
        xs[:, lanes] = x
        w = dotf(k2[...], x)
        ghs[:, lanes] = w[:cg]
        cs[...] += w[cg:, :tc] + w[cg:, tc:]
        y = dotf(x, es[1]).reshape(heads, GR, 8 * ch)
        y = jnp.sum(jnp.where(iota((heads, 1, 8 * ch), 0) == lane_c, y, 0.0), axis=0)
        rs[pl.ds(start, GR), :] = y[:, : 4 * ch]
        rs[pl.ds(start + GR, GR), :] = y[:, 4 * ch :]
        return carry

    lax.fori_loop(0, groups // 2, ahead, 0)

    for inside, own, copies, keep in segments:

        @pl.when(own)
        def _(copies=copies, keep=keep):
            keep.wait()
            for c in copies:
                c.wait_send()

        @pl.when(inside & jnp.logical_not(own))
        def _(copies=copies):
            copies[0].wait_recv()

    @pl.when(row > 0)
    def _():
        up.wait_send()
        down.wait_recv()

    @pl.when(row < n_row - 1)
    def _():
        down.wait_send()
        up.wait_recv()

    lext[0:16, :] = lbuf[0, :, :ch].astype(F32)
    lext[16 : 16 + tr, :] = proj[:, :ch].astype(F32)
    lext[16 + tr :, :] = lbuf[1, :, :ch].astype(F32)
    rext[...] = rbuf[:, ch : 2 * ch].astype(F32)

    l_sh = [lext[16 + STEP * (a - 1) : 16 + STEP * (a - 1) + tr, :] for a in range(3)]
    r_sh = [rext[16 + STEP * (b - 1) : 16 + STEP * (b - 1) + tc, :] for b in range(3)]
    a1 = sum(l_sh[a] * (taps[a][0] + taps[a][1] + taps[a][2]) for a in range(3))
    da0 = sum(l_sh[a] * taps[a][0] for a in range(3))
    da2 = sum(l_sh[a] * taps[a][2] for a in range(3))
    da = -jnp.where(col_first, da0, jnp.where(col_last, da2, jnp.zeros_like(da2)))
    b1 = sum(r_sh[b] * (taps[0][b] + taps[1][b] + taps[2][b]) for b in range(3))
    db0 = sum(r_sh[b] * taps[0][b] for b in range(3))
    db2 = sum(r_sh[b] * taps[2][b] for b in range(3))
    db = -jnp.where(row_first, db0, jnp.where(row_last, db2, jnp.zeros_like(db2)))
    rind = jnp.where(edge(row_first, row_last, iota((tr, 2 * ch), 0), tr), 1.0, 0.0).astype(BF)
    qs[...] = jnp.concatenate(
        [*split(0.5 * a1), *split(0.5 * da), jnp.ones((tr, 2 * ch), BF), rind], axis=1)
    b_parts = [p.astype(F32) for p in (*split(0.5 * b1), *split(0.5 * db))]
    ns[4 * ch :, :] = jnp.concatenate(b_parts, axis=1).T.astype(BF)
    ns[: 2 * ch, :] = jnp.ones((2 * ch, tc), BF)
    ns[2 * ch : 4 * ch, :] = jnp.where(
        edge(col_first, col_last, iota((2 * ch, tc), 1), tc), 1.0, 0.0).astype(BF)

    chunk = 32
    n = chunk // GR

    def pair(g, slot):
        start = pl.multiple_of(g * 2 * GR, 2 * GR)
        mask = cm[...].reshape(ch, GR, 8 * ch)
        for j in range(2):
            q = qs[pl.ds(start + j * GR, GR), :]
            us[slot, :, j * tc : (j + 1) * tc] = dotf((mask * q[None]).reshape(cg, 8 * ch), ns[...])
        lanes = pl.ds(pl.multiple_of(g * 2 * tc, 256), 2 * tc)
        for k in range(cg // chunk):
            rows = slice(k * chunk, (k + 1) * chunk)
            u = us[slot, rows, :]
            t = jnp.tanh(u)
            p = 1.0 + t
            h = u * p
            hid[rows, lanes] = h.astype(BF)
            gc = ghs[rows, lanes] * (p + h - h * t)
            gcs[rows, lanes] = gc.astype(BF)
            colsum[k * n : (k + 1) * n] += jnp.sum(gc.reshape(n, 2, 8, 2 * tc), axis=1)
        y = dotf(gcs[:, lanes], es[0]).reshape(ch, GR, 8 * ch)
        total = jnp.sum(jnp.where(iota((ch, 1, 8 * ch), 0) == lane_c, y, 0.0), axis=0)
        rs[pl.ds(start, GR), :] += total[:, : 4 * ch]
        rs[pl.ds(start + GR, GR), :] += total[:, 4 * ch :]

    def group(g, carry):
        pair(2 * g, 0)
        pair(2 * g + 1, 1)
        return carry

    lax.fori_loop(0, groups // 4, group, 0)
    base = jnp.sum(colsum[...], axis=1)
    base = base[:, :tc] + base[:, tc:]
    top = dotf(ecol[0], gcs[:, :tc])
    low = dotf(ecol[1], gcs[:, (groups - 1) * tc :])
    cst = jnp.concatenate([base - top, base, base - low, cs[...]], axis=0).T
    rsv = rs[...]
    eye = iota((ch, ch), 0) == iota((ch, ch), 1)
    whs = scale * jnp.concatenate([wh[...].astype(F32), jnp.zeros((ch - heads, ch), F32)], axis=0)
    zc = jnp.zeros((ch, ch), F32)

    def spread(tap):
        blocks = [[jnp.where(eye, tap(n, m), 0.0) for m in range(3)] + [zc] for n in range(3)]
        blocks.append([zc, zc, zc, whs])
        return jnp.concatenate([jnp.concatenate(b, axis=1) for b in blocks], axis=0)

    for sums, z, out, length, weights in (
        (rsv, zl, plx, tr, spread(lambda b, a: taps[a][b])),
        (cst, zr, prx, tc, spread(lambda a, b: taps[a][b])),
    ):
        z[:16, :] = jnp.zeros((16, 4 * ch), F32)
        z[16 + length :, :] = jnp.zeros((16, 4 * ch), F32)
        z[16 : 16 + length, :] = dotf(sums, weights, precision=HI)
        ext = z[8 : 24 + length, 3 * ch :]
        for n in range(3):
            ext = ext + z[12 - STEP * n : 28 - STEP * n + length, n * ch : (n + 1) * ch]
        out[...] = ext

    lanes = 4 * ch
    pp, sp = tr // 4 // n_col, 2 * ch // n_col
    colsend[...] = pack(plx[8 : 8 + tr, :]).reshape(n_col, pp, lanes)
    pad = jnp.zeros((8, 3 * ch), F32)
    halosend[0] = jnp.concatenate([plx[:8, :], pad], axis=1)
    halosend[1] = jnp.concatenate([plx[8 + tr :, :], pad], axis=1)
    pr = (tc + 16) // 4
    rowsend[...] = pack(prx[...])

    def to_col(src, dst, send, recv):
        return [remote(src(m), dst.at[col], send.at[m], recv.at[col], (row, m)) for m in col_mates]

    def to_row(src, dst, send, recv):
        return [remote(src, dst.at[row], send.at[m], recv.at[row], (m, col)) for m in row_mates]

    def from_col(src, dst, send, recv):
        return [remote(src(m), dst.at[m], send.at[m], recv.at[m], (row, m)) for m in col_mates]

    def from_row(src, dst, send, recv):
        return [remote(src, dst.at[m], send.at[m], recv.at[m], (m, col)) for m in row_mates]

    def start(copies):
        for c in copies:
            c.start()

    def arrived(copies):
        for c in copies:
            c.wait_recv()

    def sent(copies):
        for c in copies:
            c.wait_send()

    hup = remote(halosend.at[0], halorecv.at[1], h1s.at[0], h1r.at[1], (row - 1, col))
    hdown = remote(halosend.at[1], halorecv.at[0], h1s.at[1], h1r.at[0], (row + 1, col))
    p1c = (lambda m: colsend.at[m], colrecv, c1s, c1r)
    p1r = (rowsend, rowrecv, r1s, r1r)
    s1c, s1r = to_col(*p1c), to_row(*p1r)
    start(s1c)
    start(s1r)
    pl.when(row > 0)(hup.start)
    pl.when(row < n_row - 1)(hdown.start)
    prod = dotf(hid[...], xs[...], ((1,), (1,)))
    prod = jnp.sum(jnp.where(same, prod, 0.0).reshape(ch, GR, hg), axis=1)
    e_h = jnp.where(iota((hg, ch), 0) // GR == iota((hg, ch), 1), 1.0, 0.0)
    hc = dotf(prod, e_h, precision=HI)
    pc = dotf(l_sh[1], rsv[:, 3 * ch :], ((0,), (0,)), HI) + dotf(r_sh[1], cst[:, 3 * ch :], ((0,), (0,)), HI)
    small[:ch, :] = jnp.concatenate([hc, pc, jnp.zeros((ch, 2 * ch), F32)], axis=1)
    rows_out = []
    zero_l, zero_r = jnp.zeros((tr, ch), F32), jnp.zeros((tc, ch), F32)
    for a in range(3):
        rows_out.append(jnp.sum(jnp.concatenate([l_sh[a]] * 3 + [zero_l], axis=1) * rsv, axis=0, keepdims=True))
    for b in range(3):
        rows_out.append(jnp.sum(jnp.concatenate([r_sh[b]] * 3 + [zero_r], axis=1) * cst, axis=0, keepdims=True))
    small[ch : ch + 8, :] = jnp.concatenate(rows_out + [jnp.zeros((2, 4 * ch), F32)], axis=0)
    small[ch + 8 :, :] = jnp.zeros((ch - 8, 4 * ch), F32)
    smsend[...] = small[...].reshape(n_col, sp, lanes)
    p1s = (lambda m: smsend.at[m], smrecv, m1s, m1r)
    s1s = to_col(*p1s)
    start(s1s)
    arrived(from_col(*p1c))
    piece = colsend[col]
    for m in col_mates:
        piece = piece + colrecv[m]
    arrived(from_row(*p1r))
    right = rowsend[...]
    for m in row_mates:
        right = right + rowrecv[m]

    @pl.when(row > 0)
    def _():
        hup.wait_send()
        hdown.wait_recv()

    @pl.when(row < n_row - 1)
    def _():
        hdown.wait_send()
        hup.wait_recv()

    fill = [jnp.zeros((agsend.shape[0] - pp - 4 - pr, lanes), F32)] if agsend.shape[0] > pp + 4 + pr else []
    agsend[...] = jnp.concatenate(
        [right, pack(halorecv[0, :, :ch]), pack(halorecv[1, :, :ch]), piece] + fill, axis=0).astype(BF)
    p2c = (lambda m: agsend, agrecv, c2s, c2r)
    s2c = to_col(*p2c)
    start(s2c)
    arrived(from_col(*p1s))
    part = smsend[col]
    for m in col_mates:
        part = part + smrecv[m]
    spsend[...] = part
    p2r = (spsend, sprecv, r2s, r2r)
    s2r = to_row(*p2r)
    start(s2r)
    sent(s1c)
    sent(s1r)
    sent(s1s)
    arrived(from_col(*p2c))
    sent(s2c)
    agrecv[col] = agsend[...]
    gl = unpack(jnp.concatenate([agrecv[m, pr + 4 : pr + 4 + pp, :].astype(F32) for m in range(n_col)], axis=0))
    halo = sum(agrecv[m, pr : pr + 4, :].astype(F32) for m in range(n_col))
    gl = jnp.concatenate([gl[:8] + unpack(halo[:2]), gl[8:-8], gl[-8:] + unpack(halo[2:])], axis=0)
    window[...] = jnp.zeros_like(window)
    for k in range(tr // tc + 2):
        m = lax.div(row * tr, tc) - 1 + k

        @pl.when((m >= 0) & (m < n_col))
        def _(m=m, k=k):
            window[k * tc : k * tc + tc + 16, :] += unpack(agrecv[m, :pr, :].astype(F32))

    gr = window[tc + 8 : tc + 8 + tr, :]
    glb, grb = gl.astype(BF), gr.astype(BF)
    both = jnp.concatenate([gl, gr, jnp.zeros((tr, 2 * ch), F32)], axis=1).T[: 2 * ch].astype(BF)

    part = scale * dotf(both, feats[...])
    gwsend[...] = part.astype(BF)
    p3r = (gwsend, gwrecv, r3s, r3r)
    s3r = to_row(*p3r)
    start(s3r)
    arrived(from_row(*p2r))
    total = spsend[...]
    for m in row_mates:
        total = total + sprecv[m]
    sfin[col] = total
    p3c = (lambda m: sfin.at[col], sfin, c3s, c3r)
    s3c = to_col(*p3c)
    start(s3c)
    gf_out[...] = (dotf(glb, wl[...]) + dotf(grb, wr[...])).astype(BF)
    arrived(from_col(*p3c))
    sent(s3c)
    sent(s2r)
    full = jnp.concatenate([sfin[m] for m in range(n_col)], axis=0)
    hc, pc = full[:ch, :heads], full[:ch, ch : ch + heads]
    for a in range(3):
        for b in range(3):
            gk_out[3 * a + b : 3 * a + b + 1, :] = scale * (
                full[ch + a : ch + a + 1, b * ch : (b + 1) * ch]
                + full[ch + 3 + b : ch + 4 + b, a * ch : (a + 1) * ch])
    gp_out[...] = scale * scale * dotf(hc, wh[...].astype(F32), precision=HI)
    gh_out[...] = (scale * (pc + dotf(wp[...].astype(F32), hc, ((0,), (0,)), HI))).T
    arrived(from_row(*p3r))
    for m in row_mates:
        part = part + gwrecv[m].astype(F32)
    gwl_out[...] = part[:ch]
    gwr_out[...] = part[ch:]
    sent(s3r)


def move_kernel(*refs):
    sems = refs[-1]
    n = len(refs) // 2
    copies = [pltpu.make_async_copy(refs[k], refs[n + k], sems.at[k]) for k in range(n)]
    for c in copies:
        c.start()
    for c in copies:
        c.wait()


def body(bin_features, w_left, w_right, depth_kernel, w_point, w_head, cotangent):
    ch, heads = w_head.shape
    tr, tc = cotangent.shape[1:]
    n_row, n_col = lax.axis_size("row"), lax.axis_size("col")
    scale = 1.0 / math.sqrt(tr * n_row)
    cg, hg, groups = ch * GR, heads * GR, tr // GR
    d, lanes = w_left.shape[0], 4 * ch
    pp, sp, pr = tr // 4 // n_col, 2 * ch // n_col, (tc + 16) // 4
    ag = -(-(pp + 4 + pr) // 16) * 16
    vm = pl.BlockSpec(memory_space=pltpu.VMEM)
    dma = pltpu.SemaphoreType.DMA
    operands = (bin_features, w_left.T, w_right.T, depth_kernel, w_point, w_head.T, cotangent)
    outs = pl.pallas_call(
        functools.partial(tile_kernel, scale),
        out_shape=(
            pltpu.VMEM((tr, d), BF),
            pltpu.VMEM((ch, d), F32),
            pltpu.VMEM((ch, d), F32),
            pltpu.VMEM((9, ch), F32),
            pltpu.VMEM((ch, ch), F32),
            pltpu.VMEM((heads, ch), F32),
        ),
        in_specs=[pl.BlockSpec(memory_space=pltpu.HBM)] * 7,
        out_specs=(vm,) * 6,
        scratch_shapes=[
            *(pltpu.VMEM(v.shape, v.dtype) for v in operands),
            dma((7,)),
            pltpu.VMEM((cg, groups * tc), F32),
            pltpu.VMEM((tr + 32, ch), F32),
            pltpu.VMEM((tc + 32, ch), F32),
            pltpu.VMEM((tr + 16, ch), F32),
            pltpu.VMEM((tc + 16, ch), F32),
            pltpu.VMEM((2 * ch, lanes), F32),
            pltpu.VMEM((tr, 8 * ch), BF),
            pltpu.VMEM((8 * ch, tc), BF),
            pltpu.VMEM((cg + ch, hg), BF),
            pltpu.VMEM((cg, 8 * ch), BF),
            pltpu.VMEM((2, 2 * tc, 8 * ch), BF),
            pltpu.VMEM((2, ch, cg), BF),
            pltpu.VMEM((ch, 8, 2 * tc), F32),
            pltpu.VMEM((2, cg, 2 * tc), F32),
            pltpu.VMEM((tr, 4 * ch), F32),
            pltpu.VMEM((ch, tc), F32),
            pltpu.VMEM((cg, groups * tc), BF),
            pltpu.VMEM((cg, groups * tc), BF),
            pltpu.VMEM((hg, groups * tc), BF),
            pltpu.VMEM((tr + 32, 4 * ch), F32),
            pltpu.VMEM((tc + 32, 4 * ch), F32),
            pltpu.VMEM((tr, lanes), BF),
            pltpu.VMEM((2, 16, lanes), BF),
            pltpu.VMEM((tc + 32, lanes), BF),
            pltpu.VMEM((n_col, pp, lanes), F32),
            pltpu.VMEM((n_col, pp, lanes), F32),
            pltpu.VMEM((pr, lanes), F32),
            pltpu.VMEM((n_row, pr, lanes), F32),
            pltpu.VMEM((2, 8, lanes), F32),
            pltpu.VMEM((2, 8, lanes), F32),
            pltpu.VMEM((n_col, sp, lanes), F32),
            pltpu.VMEM((n_col, sp, lanes), F32),
            dma((n_col,)), dma((n_col,)),
            pltpu.VMEM((ag, lanes), BF),
            pltpu.VMEM((n_col, ag, lanes), BF),
            pltpu.VMEM((sp, lanes), F32),
            pltpu.VMEM((n_row, sp, lanes), F32),
            pltpu.VMEM((n_col, sp, lanes), F32),
            pltpu.VMEM((2 * ch, d), BF),
            pltpu.VMEM((n_row, 2 * ch, d), BF),
            pltpu.VMEM((tr + 2 * tc + 16, ch), F32),
            dma((3, n_row)), dma((3,)), dma((2,)), dma((2,)),
            dma((n_col,)), dma((n_col,)), dma((n_row,)), dma((n_row,)), dma((2,)), dma((2,)),
            dma((n_col,)), dma((n_col,)), dma((n_row,)), dma((n_row,)),
            dma((n_col,)), dma((n_col,)), dma((n_row,)), dma((n_row,)),
            dma((3,)),
        ],
        compiler_params=pltpu.CompilerParams(
            vmem_limit_bytes=63 * 1024 * 1024, collective_id=0, has_side_effects=True),
    )(*operands)
    hbm = pl.BlockSpec(memory_space=pltpu.HBM)
    gf, gwl, gwr, gk, gp, gh = pl.pallas_call(
        move_kernel,
        out_shape=tuple(jax.ShapeDtypeStruct(v.shape, v.dtype) for v in outs),
        in_specs=[vm] * 6,
        out_specs=(hbm,) * 6,
        scratch_shapes=[dma((6,))],
        compiler_params=pltpu.CompilerParams(vmem_limit_bytes=16 * 1024 * 1024),
    )(*outs)
    return gf, gwl.T, gwr.T, gk, gp, gh.T


def solution(mesh):
    return jax.shard_map(
        body,
        mesh=mesh,
        in_specs=(P("row", None), P(), P(), P(), P(), P(), P(None, "row", "col")),
        out_specs=(P("row", None), P(), P(), P(), P(), P()),
        check_vma=False,
    )
```
